1024 devices in a mesh: dp: 2 (over x_lo), hid: 64 (over z, core), inp: 8 (over y, x_hi).
Axes of the slice: x: 4 (x_hi: 2, x_lo: 2; x = x_hi * 2 + x_lo), y: 4, z: 32, core: 2. Of those that a mesh axis runs over, the one named last changes fastest.
Arguments:
- out_grad: bfloat16 [512, 16384], P(('dp', 'hid'), 'inp'), may hold values from -6 to 6
- gate_act: bfloat16 [512, 32768], P('dp', 'hid'), may hold values from -6 to 6
- up_act: bfloat16 [512, 32768], P('dp', 'hid'), may hold values from -6 to 6
- frames: bfloat16 [512, 1280], P('dp', 'hid'), may hold values from -0.59765625 to 0.59765625
- w_gate: bfloat16 [16384, 32768], P('inp', 'hid'), may hold values from -0.046875 to 0.046875
- w_up: bfloat16 [16384, 32768], P('inp', 'hid'), may hold values from -0.046875 to 0.046875
- w_down: bfloat16 [32768, 16384], P('hid', 'inp'), may hold values from -0.03125 to 0.03125
Outputs:
- input_grad: bfloat16 [512, 16384], P(('dp', 'hid'), 'inp')
- adapter_grad: float32 [1280, 16384], P('hid', 'inp')
The draws below stay inside these ranges and needn't reach their ends.
All inputs are finite; a program needn't handle non-finite values.
Results may differ from the reference program's by a relative error of at most 0.0049.
Values may be sent and summed in bfloat16 or wider, within the bound.
A program may use at most 32 MiB of HBM per device.

```python
import jax
import jax.numpy as jnp
from jax import lax

D = 16384
FF_DEV = 512
FF = 32768
E = 1280
ROWS = 512


def level_of(key, shape, split, least, top_value):
    loudness, own = 1.0, jax.random.fold_in(key, 6)
    for axis_at, shards_of in split:
        draws = jnp.exp(jax.random.uniform(jax.random.fold_in(own, axis_at), (shards_of,), jnp.float32, least / len(split), top_value / len(split)))
        loudness = loudness * jnp.repeat(draws, shape[axis_at] // shards_of).reshape([-1 if axis == axis_at else 1 for axis in range(len(shape))])
    return loudness


def gaussian(own_key, shape, spread, reach, split=(), dtype=jnp.bfloat16):
    array = spread * jax.random.normal(own_key, shape, jnp.float32)
    if split:
        array = array * level_of(own_key, shape, split, -0.22, 0.18)
    return jnp.clip(array, -reach, reach).astype(dtype)


def setup_inputs(seed: int = 0) -> dict:
    splits = jax.random.split(jax.random.key(seed), 8)
    return {
        "out_grad": gaussian(splits[0], (ROWS, D), 1.0, 6.0, ((0, 128), (1, 8))),
        "gate_act": gaussian(splits[1], (ROWS, FF), 1.0, 6.0, ((0, 2), (1, 64))),
        "up_act": gaussian(splits[2], (ROWS, FF), 1.0, 6.0, ((0, 2), (1, 64))),
        "frames": gaussian(splits[3], (ROWS, E), 0.1, 0.59765625, ((0, 2), (1, 64))),
        "w_gate": gaussian(splits[4], (D, FF), D ** -0.5, 0.046875, ((0, 8), (1, 64))),
        "w_up": gaussian(splits[5], (D, FF), D ** -0.5, 0.046875, ((0, 8), (1, 64))),
        "w_down": gaussian(splits[6], (FF, D), FF ** -0.5, 0.03125, ((0, 64), (1, 8))),
    }


def contract_last(left, right):
    return lax.dot_general(left, right, (((1,), (1,)), ((), ())), preferred_element_type=jnp.float32)


def reference(out_grad, gate_act, up_act, frames, w_gate, w_up, w_down):
    def block_step(index, total):
        start = (index * FF_DEV).astype(jnp.int32)
        down_block = lax.dynamic_slice_in_dim(w_down, start, FF_DEV, 0)
        gate_block = lax.dynamic_slice_in_dim(w_gate, start, FF_DEV, 1)
        up_block = lax.dynamic_slice_in_dim(w_up, start, FF_DEV, 1)
        gate = lax.dynamic_slice_in_dim(gate_act, start, FF_DEV, 1).astype(jnp.float32)
        upper = lax.dynamic_slice_in_dim(up_act, start, FF_DEV, 1).astype(jnp.float32)
        hidden_grad = contract_last(out_grad, down_block)
        sigma = jax.nn.sigmoid(gate)
        gate_grad = (hidden_grad * upper * sigma * (1.0 + gate * (1.0 - sigma))).astype(jnp.bfloat16)
        up_grad = (hidden_grad * gate * sigma).astype(jnp.bfloat16)
        return total + contract_last(gate_grad, gate_block) + contract_last(up_grad, up_block)

    start_total = jnp.zeros((out_grad.shape[0], out_grad.shape[1]), jnp.float32)
    summed = lax.fori_loop(0, FF // FF_DEV, block_step, start_total)
    input_grad = summed.astype(jnp.bfloat16)
    adapter_grad = lax.dot_general(frames, input_grad, (((0,), (0,)), ((), ())), preferred_element_type=jnp.float32)
    return input_grad, adapter_grad
```

```python
import functools

import jax
import jax.numpy as jnp
from jax import lax
from jax.experimental import pallas as pl
from jax.experimental.pallas import tpu as pltpu
from jax.sharding import PartitionSpec as P

MESH = pl.DeviceIdType.MESH
BF = jnp.bfloat16
F32 = jnp.float32
NEAR = 4


def dot_nt(a, b):
    return lax.dot_general(a, b, (((1,), (1,)), ((), ())), preferred_element_type=F32)


def dot_nn(a, b):
    return lax.dot_general(a, b, (((1,), (0,)), ((), ())), preferred_element_type=F32)


def body(Z, N, *refs):
    (og, gact, uact, frames, wg, wu, wd, ig_out, ad_out,
     abuf, dbuf, full, hpart, hrecv, gu, gact_v, uact_v, wg_v, wu_v, wd_v,
     sibf, sibr, pown, csend, cnear, fsend, cfar, eloc, erem,
     lsem, a_sem, d_sem, hs, hr, gs, gr, ss, sr, ns, nr, fs, fr, es, er) = refs
    K = Z // NEAR
    hid = lax.axis_index("hid")
    z = hid // 2
    c = hid % 2
    inp = lax.axis_index("inp")
    dp = lax.axis_index("dp")
    r = z % NEAR
    k = z // NEAR
    sib = {"hid": 2 * z + 1 - c}
    peer = {"dp": 1 - dp}

    def chip(d):
        return {"hid": 2 * ((z + d + 2 * Z) % Z) + c}

    def chip_at(w):
        return {"hid": 2 * w + c}

    def ring(j):
        return {"inp": (inp + j) % N}

    barrier = pltpu.get_barrier_semaphore()
    offsets = sorted({NEAR * m for m in range(1, K)} | {1, 2, Z - 1, Z - 2})
    for d in offsets:
        pl.semaphore_signal(barrier, inc=1, device_id=chip(d), device_id_type=MESH)
    for j in range(1, N):
        pl.semaphore_signal(barrier, inc=1, device_id=ring(j), device_id_type=MESH)
    pl.semaphore_signal(barrier, inc=1, device_id=sib, device_id_type=MESH)
    pl.semaphore_signal(barrier, inc=1, device_id=peer, device_id_type=MESH)

    mine32 = pl.ds(pl.multiple_of(inp * 32, 32), 32)
    local = [
        pltpu.make_async_copy(og, abuf.at[r, c, k], lsem.at[0]),
        pltpu.make_async_copy(wd, wd_v, lsem.at[1]),
        pltpu.make_async_copy(gact.at[mine32], gact_v, lsem.at[2]),
        pltpu.make_async_copy(uact.at[mine32], uact_v, lsem.at[3]),
        pltpu.make_async_copy(wg, wg_v, lsem.at[4]),
        pltpu.make_async_copy(wu, wu_v, lsem.at[5]),
    ]
    for q in local:
        q.start()

    o = lax.broadcasted_iota(jnp.int32, (256, 256), 0)
    i = lax.broadcasted_iota(jnp.int32, (256, 256), 1)
    to = ((i // 4) % 4) * 64 + ((i // 16) % 2) * 32 + (i // 64) * 8 + ((i // 32) % 2) * 4 + i % 4
    perm = jnp.where(o == to, 1.0, 0.0).astype(BF)
    rows = Z * 8
    row = lax.broadcasted_iota(jnp.int32, (rows, 2 * rows), 0)
    col = lax.broadcasted_iota(jnp.int32, (rows, 2 * rows), 1)
    src = 8 * (NEAR * ((col // 16) % K) + col // (16 * K)) + col % 8
    half = (col // 8) % 2
    fr_t = frames[...]
    f0 = dot_nn(fr_t, jnp.where((row == src) & (half == 0), 1.0, 0.0).astype(BF)).astype(BF)
    f1 = dot_nn(fr_t, jnp.where((row == src) & (half == 1), 1.0, 0.0).astype(BF)).astype(BF)

    local[0].wait()
    pl.semaphore_wait(barrier, len(offsets) + N + 1)

    sent = []

    def remote(s, d, send, recv, dev):
        return pltpu.make_async_remote_copy(
            src_ref=s, dst_ref=d, send_sem=send, recv_sem=recv, device_id=dev, device_id_type=MESH
        )

    def launch(*args):
        q = remote(*args)
        q.start()
        sent.append(q)

    def gather(buf, sem):
        mine = buf.at[r, c, k]
        for m in sorted(range(1, K), key=lambda m: -min(m, K - m)):
            launch(mine, mine, sem.at[0, m], sem.at[1, m], chip(NEAR * m))
        for m in sorted(range(1, K), key=lambda m: min(m, K - m)):
            got = buf.at[r, c, (k - m + K) % K]
            remote(got, got, sem.at[0, m], sem.at[1, m], chip(NEAR * m)).wait_recv()
        group = buf.at[r, c]
        two = 2 - 4 * c
        for n, d in enumerate((two, 1, -1)):
            launch(group, group, sem.at[2, n], sem.at[3, n], chip(d))
        launch(group, group, sem.at[4, 3], sem.at[5, 3], sib)
        for n, d in ((1, 1), (2, -1), (0, two)):
            got = buf.at[(r - d + NEAR) % NEAR, c]
            remote(got, got, sem.at[2, n], sem.at[3, n], chip(d)).wait_recv()
            launch(got, got, sem.at[4, n], sem.at[5, n], sib)
        for n, d in ((3, 0), (1, 1), (2, -1), (0, 2)):
            got = buf.at[(r - d + NEAR) % NEAR, 1 - c]
            remote(got, got, sem.at[4, n], sem.at[5, n], sib).wait_recv()

    gather(abuf, a_sem)

    for j in range(K // 2):
        rows_in = abuf[:, :, 2 * j : 2 * j + 2].reshape(256, 512)
        out = dot_nn(perm, rows_in).astype(BF)
        for q in range(4):
            full[64 * j : 64 * j + 64, 512 * q : 512 * q + 512] = out[64 * q : 64 * q + 64]
    local[1].wait()
    hpart[...] = dot_nt(full[...], wd_v[...]).reshape(hpart.shape)

    for j in range(1, N):
        launch(hpart.at[(inp + j) % N], hrecv.at[j - 1], hs.at[j], hr.at[j], ring(j))
    local[2].wait()
    local[3].wait()
    gate = gact_v[...].astype(F32)
    upper = uact_v[...].astype(F32)
    sigma = jax.nn.sigmoid(gate)
    total = hpart[inp]
    for j in range(1, N):
        remote(hpart.at[(inp + j) % N], hrecv.at[j - 1], hs.at[j], hr.at[j], ring(j)).wait_recv()
        total = total + hrecv[j - 1]
    gu[inp, 0] = (total * upper * sigma * (1.0 + gate * (1.0 - sigma))).astype(BF)
    gu[inp, 1] = (total * gate * sigma).astype(BF)
    for j in range(1, N):
        launch(gu.at[inp], gu.at[inp], gs.at[j], gr.at[j], ring(j))
    local[4].wait()
    local[5].wait()
    for j in range(1, N):
        got = gu.at[(inp - j + N) % N]
        remote(got, got, gs.at[j], gr.at[j], ring(j)).wait_recv()

    gg = gu[:, 0].reshape(256, 512)
    ug = gu[:, 1].reshape(256, 512)

    def part(start):
        w = pl.ds(pl.multiple_of(start, 512), 512)
        return (dot_nt(gg, wg_v[w, :]) + dot_nt(ug, wu_v[w, :])).reshape(K, NEAR, 8, 512)

    for h in range(2):
        sibf[h] = part((1 - c) * 1024 + h * 512)
        launch(sibf.at[h], sibr.at[h], ss.at[h], sr.at[h], sib)
    for h in range(2):
        pown[h] = part(c * 1024 + h * 512)
    for h in range(2):
        remote(sibf.at[h], sibr.at[h], ss.at[h], sr.at[h], sib).wait_recv()
        for s in range(NEAR):
            both = pown[h, :, s] + sibr[h, :, s]
            pown[h, :, s] = both
    for s in range(NEAR):
        csend[s] = jnp.concatenate([pown[0, :, s], pown[1, :, s]], axis=1).astype(BF)

    two = 2 - 4 * c
    for n, d in enumerate((two, 1, -1)):
        launch(csend.at[(r + d + NEAR) % NEAR], cnear.at[n], ns.at[n], nr.at[n], chip(d))
    acc = jnp.concatenate([pown[0, :, r], pown[1, :, r]], axis=1)
    for n, d in ((1, 1), (2, -1), (0, two)):
        remote(csend.at[0], cnear.at[n], ns.at[n], nr.at[n], chip(d)).wait_recv()
        acc = acc + cnear[n].astype(F32)
    fsend[...] = acc.astype(BF)
    for m in sorted(range(1, K), key=lambda m: -min(m, K - m)):
        launch(fsend.at[(k + m) % K], cfar.at[m - 1], fs.at[m], fr.at[m], chip(NEAR * m))
    total = jnp.concatenate([pown[0, k, r], pown[1, k, r]], axis=0)
    for n in range(3):
        total = total + cnear[n, k].astype(F32)
    for m in sorted(range(1, K), key=lambda m: min(m, K - m)):
        remote(fsend.at[0], cfar.at[m - 1], fs.at[m], fr.at[m], chip(NEAR * m)).wait_recv()
        total = total + cfar[m - 1].astype(F32)
    dbuf[r, c, k] = total.astype(BF)

    gather(dbuf, d_sem)

    for a in range(2):
        blk = dbuf[r, a, k].astype(F32)
        ig_out[:, 1024 * a : 1024 * a + 512] = blk[0:8]
        ig_out[:, 1024 * a + 512 : 1024 * a + 1024] = blk[8:16]
        x = dbuf[:, a].reshape(2 * rows, 512)
        eloc[0:20, 1024 * a : 1024 * a + 512] = dot_nn(f0, x)
        eloc[0:20, 1024 * a + 512 : 1024 * a + 1024] = dot_nn(f1, x)
    eloc[20:24, :] = jnp.zeros((4, 2048), F32)
    launch(eloc, erem, es, er, peer)
    remote(eloc, erem, es, er, peer).wait_recv()
    ad_out[...] = eloc[0:20, :] + erem[0:20, :]
    for q in sent:
        q.wait_send()


def per_device(Z, N, out_grad, gate_act, up_act, frames, w_gate, w_up, w_down):
    K = Z // NEAR
    og = out_grad.reshape(4, 4, 512).transpose(1, 0, 2).reshape(16, 512)
    hbm = pl.BlockSpec(memory_space=pl.ANY)
    vmem = pl.BlockSpec(memory_space=pltpu.VMEM)
    dma = pltpu.SemaphoreType.DMA
    ig8, ad = pl.pallas_call(
        functools.partial(body, Z, N),
        out_shape=(jax.ShapeDtypeStruct((8, 2048), F32), jax.ShapeDtypeStruct((20, 2048), F32)),
        in_specs=[hbm, hbm, hbm, vmem, hbm, hbm, hbm],
        out_specs=(vmem, vmem),
        scratch_shapes=[
            pltpu.VMEM((NEAR, 2, K, 16, 512), BF),
            pltpu.VMEM((NEAR, 2, K, 16, 512), BF),
            pltpu.VMEM((256, 2048), BF),
            pltpu.VMEM((N, 32, 512), F32),
            pltpu.VMEM((N - 1, 32, 512), F32),
            pltpu.VMEM((N, 2, 32, 512), BF),
            pltpu.VMEM((32, 512), BF),
            pltpu.VMEM((32, 512), BF),
            pltpu.VMEM((2048, 512), BF),
            pltpu.VMEM((2048, 512), BF),
            pltpu.VMEM((512, 2048), BF),
            pltpu.VMEM((2, K, NEAR, 8, 512), F32),
            pltpu.VMEM((2, K, NEAR, 8, 512), F32),
            pltpu.VMEM((2, K, NEAR, 8, 512), F32),
            pltpu.VMEM((NEAR, K, 16, 512), BF),
            pltpu.VMEM((3, K, 16, 512), BF),
            pltpu.VMEM((K, 16, 512), BF),
            pltpu.VMEM((K - 1, 16, 512), BF),
            pltpu.VMEM((24, 2048), F32),
            pltpu.VMEM((24, 2048), F32),
            dma((6,)),
            dma((6, 8)),
            dma((6, 8)),
            dma((8,)),
            dma((8,)),
            dma((8,)),
            dma((8,)),
            dma((2,)),
            dma((2,)),
            dma((3,)),
            dma((3,)),
            dma((8,)),
            dma((8,)),
            dma,
            dma,
        ],
        compiler_params=pltpu.CompilerParams(
            collective_id=0, has_side_effects=True, vmem_limit_bytes=48 * 1024 * 1024
        ),
        cost_estimate=pl.CostEstimate(flops=1_700_000_000, bytes_accessed=8_000_000, transcendentals=0),
    )(og, gate_act, up_act, frames.T, w_gate, w_up, w_down)
    core = lax.axis_index("hid") % 2
    input_grad = lax.dynamic_slice_in_dim(ig8, core * 4, 4, 0).astype(BF)
    return input_grad, ad


def solution(mesh):
    Z = mesh.shape["hid"] // 2
    N = mesh.shape["inp"]
    return jax.shard_map(
        functools.partial(per_device, Z, N),
        mesh=mesh,
        in_specs=(
            P(("dp", "hid"), "inp"),
            P("dp", "hid"),
            P("dp", "hid"),
            P("dp", "hid"),
            P("inp", "hid"),
            P("inp", "hid"),
            P("hid", "inp"),
        ),
        out_specs=(P(("dp", "hid"), "inp"), P("hid", "inp")),
        check_vma=False,
    )
```

```python
import functools

import jax
import jax.numpy as jnp
from jax import lax
from jax.experimental import pallas as pl
from jax.experimental.pallas import tpu as pltpu
from jax.sharding import PartitionSpec as P

MESH = pl.DeviceIdType.MESH
BF = jnp.bfloat16
F32 = jnp.float32
NEAR = 4


def dot_nt(a, b):
    return lax.dot_general(a, b, (((1,), (1,)), ((), ())), preferred_element_type=F32)


def dot_nn(a, b):
    return lax.dot_general(a, b, (((1,), (0,)), ((), ())), preferred_element_type=F32)


def body(Z, N, *refs):
    (og, gact, uact, frames, wg, wu, wd, ig_out, ad_out,
     abuf, dbuf, full, hpart, hrecv, gu, gact_v, uact_v, wg_v, wu_v, wd_v,
     sibf, sibr, pown, csend, cnear, fsend, cfar, eloc, erem,
     lsem, a_sem, d_sem, hs, hr, gs, gr, ss, sr, ns, nr, fs, fr, es, er) = refs
    K = Z // NEAR
    hid = lax.axis_index("hid")
    z = hid // 2
    c = hid % 2
    inp = lax.axis_index("inp")
    dp = lax.axis_index("dp")
    r = z % NEAR
    k = z // NEAR
    sib = {"hid": 2 * z + 1 - c}
    peer = {"dp": 1 - dp}

    def chip(d):
        return {"hid": 2 * ((z + d + 2 * Z) % Z) + c}

    def chip_at(w):
        return {"hid": 2 * w + c}

    def ring(j):
        return {"inp": (inp + j) % N}

    barrier = pltpu.get_barrier_semaphore()
    offsets = (NEAR, Z - NEAR, 1, Z - 1, 2, Z - 2)
    for d in offsets:
        pl.semaphore_signal(barrier, inc=1, device_id=chip(d), device_id_type=MESH)
    for j in range(1, N):
        pl.semaphore_signal(barrier, inc=1, device_id=ring(j), device_id_type=MESH)
    pl.semaphore_signal(barrier, inc=1, device_id=sib, device_id_type=MESH)
    pl.semaphore_signal(barrier, inc=1, device_id=peer, device_id_type=MESH)

    mine32 = pl.ds(pl.multiple_of(inp * 32, 32), 32)
    local = [
        pltpu.make_async_copy(og, abuf.at[r, c, k], lsem.at[0]),
        pltpu.make_async_copy(wd, wd_v, lsem.at[1]),
        pltpu.make_async_copy(gact.at[mine32], gact_v, lsem.at[2]),
        pltpu.make_async_copy(uact.at[mine32], uact_v, lsem.at[3]),
        pltpu.make_async_copy(wg, wg_v, lsem.at[4]),
        pltpu.make_async_copy(wu, wu_v, lsem.at[5]),
    ]
    for q in local:
        q.start()

    local[0].wait()
    pl.semaphore_wait(barrier, len(offsets) + N + 1)

    sent = []

    def remote(s, d, send, recv, dev):
        return pltpu.make_async_remote_copy(
            src_ref=s, dst_ref=d, send_sem=send, recv_sem=recv, device_id=dev, device_id_type=MESH
        )

    def launch(*args):
        q = remote(*args)
        q.start()
        sent.append(q)

    two = 2 - 4 * c
    near = (two, 1, -1)
    arrivals = []
    for m in range(1, K // 2 + 1):
        arrivals += [m, -m] if m < K - m else [m]

    def far_step(buf, sem, m):
        blk = buf.at[r, c, (k - m + K) % K]
        if 0 <= m < K // 2:
            launch(blk, blk, sem.at[0, m + 1], sem.at[1, m + 1], chip(NEAR))
        if -(K // 2 - 1) < m <= 0:
            launch(blk, blk, sem.at[0, (m - 1) % K], sem.at[1, (m - 1) % K], chip(-NEAR))
        for n, d in enumerate(near):
            launch(blk, blk, sem.at[2 + 2 * n, m % K], sem.at[3 + 2 * n, m % K], chip(d))

    def gather(buf, sem):
        for m in arrivals:
            got = buf.at[r, c, (k - m + K) % K]
            remote(got, got, sem.at[0, m % K], sem.at[1, m % K], chip(NEAR)).wait_recv()
            far_step(buf, sem, m)
        group = buf.at[r, c]
        launch(group, group, sem.at[8, 3], sem.at[9, 3], sib)
        for n, d in ((1, 1), (2, -1), (0, two)):
            s = (r - d + NEAR) % NEAR
            for m in [0] + arrivals:
                got = buf.at[s, c, ((z - d + Z) // NEAR - m + K) % K]
                remote(got, got, sem.at[2 + 2 * n, m % K], sem.at[3 + 2 * n, m % K], chip(d)).wait_recv()
            got = buf.at[s, c]
            launch(got, got, sem.at[8, n], sem.at[9, n], sib)
        for n, d in ((3, 0), (1, 1), (2, -1), (0, 2)):
            got = buf.at[(r - d + NEAR) % NEAR, 1 - c]
            remote(got, got, sem.at[8, n], sem.at[9, n], sib).wait_recv()

    far_step(abuf, a_sem, 0)

    o = lax.broadcasted_iota(jnp.int32, (256, 256), 0)
    i = lax.broadcasted_iota(jnp.int32, (256, 256), 1)
    to = ((i // 4) % 4) * 64 + ((i // 16) % 2) * 32 + (i // 64) * 8 + ((i // 32) % 2) * 4 + i % 4
    perm = jnp.where(o == to, 1.0, 0.0).astype(BF)
    rows = Z * 8
    row = lax.broadcasted_iota(jnp.int32, (rows, 2 * rows), 0)
    col = lax.broadcasted_iota(jnp.int32, (rows, 2 * rows), 1)
    src = 8 * (NEAR * ((col // 16) % K) + col // (16 * K)) + col % 8
    half = (col // 8) % 2
    fr_t = frames[...]
    f0 = dot_nn(fr_t, jnp.where((row == src) & (half == 0), 1.0, 0.0).astype(BF)).astype(BF)
    f1 = dot_nn(fr_t, jnp.where((row == src) & (half == 1), 1.0, 0.0).astype(BF)).astype(BF)

    gather(abuf, a_sem)

    for j in range(K // 2):
        rows_in = abuf[:, :, 2 * j : 2 * j + 2].reshape(256, 512)
        out = dot_nn(perm, rows_in).astype(BF)
        for q in range(4):
            full[64 * j : 64 * j + 64, 512 * q : 512 * q + 512] = out[64 * q : 64 * q + 64]
    local[1].wait()
    hpart[...] = dot_nt(full[...], wd_v[...]).reshape(hpart.shape)

    for j in range(1, N):
        launch(hpart.at[(inp + j) % N], hrecv.at[j - 1], hs.at[j], hr.at[j], ring(j))
    local[2].wait()
    local[3].wait()
    gate = gact_v[...].astype(F32)
    upper = uact_v[...].astype(F32)
    sigma = jax.nn.sigmoid(gate)
    total = hpart[inp]
    for j in range(1, N):
        remote(hpart.at[(inp + j) % N], hrecv.at[j - 1], hs.at[j], hr.at[j], ring(j)).wait_recv()
        total = total + hrecv[j - 1]
    gu[inp, 0] = (total * upper * sigma * (1.0 + gate * (1.0 - sigma))).astype(BF)
    gu[inp, 1] = (total * gate * sigma).astype(BF)
    for j in range(1, N):
        launch(gu.at[inp], gu.at[inp], gs.at[j], gr.at[j], ring(j))
    local[4].wait()
    local[5].wait()
    for j in range(1, N):
        got = gu.at[(inp - j + N) % N]
        remote(got, got, gs.at[j], gr.at[j], ring(j)).wait_recv()

    gg = gu[:, 0].reshape(256, 512)
    ug = gu[:, 1].reshape(256, 512)

    def part(start):
        w = pl.ds(pl.multiple_of(start, 512), 512)
        return (dot_nt(gg, wg_v[w, :]) + dot_nt(ug, wu_v[w, :])).reshape(Z, 8, 512)

    for h in range(2):
        sibf[h] = part((1 - c) * 1024 + h * 512)
        launch(sibf.at[h], sibr.at[h], ss.at[h], sr.at[h], sib)
    for h in range(2):
        pown[h] = part(c * 1024 + h * 512)
    for h in range(2):
        remote(sibf.at[h], sibr.at[h], ss.at[h], sr.at[h], sib).wait_recv()
        pown[h] = pown[h] + sibr[h]

    order = sorted(range(K), key=lambda m: -min(m, K - m))
    cut = K // 2

    def rows_of(w):
        w = (w + 2 * Z) % Z
        return jnp.concatenate([pown[0, w], pown[1, w]], axis=0)

    for p in range(2):
        part_m = pl.ds(cut * p, cut)
        for n, d in enumerate(near):
            for t in range(cut * p, cut * p + cut):
                csend[n, t] = rows_of(z + d + NEAR * order[t]).astype(BF)
            launch(csend.at[n, part_m], cnear.at[n, part_m], ns.at[n, p], nr.at[n, p], chip(d))
    for p in range(2):
        part_m = pl.ds(cut * p, cut)
        for n, d in ((1, 1), (2, -1), (0, two)):
            remote(csend.at[n, part_m], cnear.at[n, part_m], ns.at[n, p], nr.at[n, p], chip(d)).wait_recv()
        for t in range(cut * p, cut * p + cut):
            m = order[t]
            total = rows_of(z + NEAR * m)
            for n in range(3):
                total = total + cnear[n, t].astype(F32)
            if m:
                fsend[m] = total.astype(BF)
                launch(fsend.at[m], cfar.at[m], fs.at[m], fr.at[m], chip(NEAR * m))
    for m in sorted(range(1, K), key=lambda m: min(m, K - m)):
        remote(fsend.at[m], cfar.at[m], fs.at[m], fr.at[m], chip(NEAR * m)).wait_recv()
        total = total + cfar[m].astype(F32)
    dbuf[r, c, k] = total.astype(BF)

    far_step(dbuf, d_sem, 0)
    gather(dbuf, d_sem)

    for a in range(2):
        x = dbuf[:, a].reshape(2 * rows, 512)
        eloc[a, 0:20, 0:512] = dot_nn(f0, x)
        eloc[a, 0:20, 512:1024] = dot_nn(f1, x)
        eloc[a, 20:24, :] = jnp.zeros((4, 1024), F32)
        launch(eloc.at[a], erem.at[a], es.at[a], er.at[a], peer)
    for a in range(2):
        blk = dbuf[r, a, k].astype(F32)
        ig_out[:, 1024 * a : 1024 * a + 512] = blk[0:8]
        ig_out[:, 1024 * a + 512 : 1024 * a + 1024] = blk[8:16]
    for a in range(2):
        remote(eloc.at[a], erem.at[a], es.at[a], er.at[a], peer).wait_recv()
        ad_out[:, 1024 * a : 1024 * a + 1024] = eloc[a, 0:20, :] + erem[a, 0:20, :]
    for q in sent:
        q.wait_send()


def per_device(Z, N, out_grad, gate_act, up_act, frames, w_gate, w_up, w_down):
    K = Z // NEAR
    og = out_grad.reshape(4, 4, 512).transpose(1, 0, 2).reshape(16, 512)
    hbm = pl.BlockSpec(memory_space=pl.ANY)
    vmem = pl.BlockSpec(memory_space=pltpu.VMEM)
    dma = pltpu.SemaphoreType.DMA
    ig8, ad = pl.pallas_call(
        functools.partial(body, Z, N),
        out_shape=(jax.ShapeDtypeStruct((8, 2048), F32), jax.ShapeDtypeStruct((20, 2048), F32)),
        in_specs=[hbm, hbm, hbm, vmem, hbm, hbm, hbm],
        out_specs=(vmem, vmem),
        scratch_shapes=[
            pltpu.VMEM((NEAR, 2, K, 16, 512), BF),
            pltpu.VMEM((NEAR, 2, K, 16, 512), BF),
            pltpu.VMEM((256, 2048), BF),
            pltpu.VMEM((N, 32, 512), F32),
            pltpu.VMEM((N - 1, 32, 512), F32),
            pltpu.VMEM((N, 2, 32, 512), BF),
            pltpu.VMEM((32, 512), BF),
            pltpu.VMEM((32, 512), BF),
            pltpu.VMEM((2048, 512), BF),
            pltpu.VMEM((2048, 512), BF),
            pltpu.VMEM((512, 2048), BF),
            pltpu.VMEM((2, Z, 8, 512), F32),
            pltpu.VMEM((2, Z, 8, 512), F32),
            pltpu.VMEM((2, Z, 8, 512), F32),
            pltpu.VMEM((3, K, 16, 512), BF),
            pltpu.VMEM((3, K, 16, 512), BF),
            pltpu.VMEM((K, 16, 512), BF),
            pltpu.VMEM((K, 16, 512), BF),
            pltpu.VMEM((2, 24, 1024), F32),
            pltpu.VMEM((2, 24, 1024), F32),
            dma((6,)),
            dma((10, 8)),
            dma((10, 8)),
            dma((8,)),
            dma((8,)),
            dma((8,)),
            dma((8,)),
            dma((2,)),
            dma((2,)),
            dma((3, 2)),
            dma((3, 2)),
            dma((8,)),
            dma((8,)),
            dma((2,)),
            dma((2,)),
        ],
        compiler_params=pltpu.CompilerParams(
            collective_id=0, has_side_effects=True, vmem_limit_bytes=60 * 1024 * 1024
        ),
        cost_estimate=pl.CostEstimate(flops=1_700_000_000, bytes_accessed=8_000_000, transcendentals=0),
    )(og, gate_act, up_act, frames.T, w_gate, w_up, w_down)
    core = lax.axis_index("hid") % 2
    input_grad = lax.dynamic_slice_in_dim(ig8, core * 4, 4, 0).astype(BF)
    return input_grad, ad


def solution(mesh):
    Z = mesh.shape["hid"] // 2
    N = mesh.shape["inp"]
    return jax.shard_map(
        functools.partial(per_device, Z, N),
        mesh=mesh,
        in_specs=(
            P(("dp", "hid"), "inp"),
            P("dp", "hid"),
            P("dp", "hid"),
            P("dp", "hid"),
            P("inp", "hid"),
            P("inp", "hid"),
            P("hid", "inp"),
        ),
        out_specs=(P(("dp", "hid"), "inp"), P("hid", "inp")),
        check_vma=False,
    )
```

```python
import functools

import jax
import jax.numpy as jnp
from jax import lax
from jax.experimental import pallas as pl
from jax.experimental.pallas import tpu as pltpu
from jax.sharding import PartitionSpec as P

MESH = pl.DeviceIdType.MESH
BF = jnp.bfloat16
F32 = jnp.float32
NEAR = 4


def dot_nt(a, b):
    return lax.dot_general(a, b, (((1,), (1,)), ((), ())), preferred_element_type=F32)


def dot_nn(a, b):
    return lax.dot_general(a, b, (((1,), (0,)), ((), ())), preferred_element_type=F32)


def body(Z, N, *refs):
    (og, gact, uact, frames, wg, wu, wd, ig_out, ad_out,
     abuf, dbuf, full, hpart, hsend, hrecv, hsum, gate_by, up_by, gu, gact_v, uact_v, wg_v, wu_v, wd_v,
     sibf, sibr, pown, csend, cnear, fsend, cfar, eloc, erem,
     lsem, a_sem, d_sem, hs, hr, gs, gr, ss, sr, ns, nr, fs, fr, es, er) = refs
    K = Z // NEAR
    hid = lax.axis_index("hid")
    z = hid // 2
    c = hid % 2
    inp = lax.axis_index("inp")
    dp = lax.axis_index("dp")
    r = z % NEAR
    k = z // NEAR
    sib = {"hid": 2 * z + 1 - c}
    peer = {"dp": 1 - dp}

    def chip(d):
        return {"hid": 2 * ((z + d + 2 * Z) % Z) + c}

    def chip_at(w):
        return {"hid": 2 * w + c}

    def ring(j):
        return {"inp": (inp + j) % N}

    barrier = pltpu.get_barrier_semaphore()
    offsets = (NEAR, Z - NEAR, 1, Z - 1, 2, Z - 2)
    for d in offsets:
        pl.semaphore_signal(barrier, inc=1, device_id=chip(d), device_id_type=MESH)
    for j in range(1, N):
        pl.semaphore_signal(barrier, inc=1, device_id=ring(j), device_id_type=MESH)
    pl.semaphore_signal(barrier, inc=1, device_id=sib, device_id_type=MESH)
    pl.semaphore_signal(barrier, inc=1, device_id=peer, device_id_type=MESH)

    local = [
        pltpu.make_async_copy(wd, wd_v, lsem.at[0]),
        pltpu.make_async_copy(gact, gact_v, lsem.at[1]),
        pltpu.make_async_copy(uact, uact_v, lsem.at[2]),
        pltpu.make_async_copy(wg, wg_v, lsem.at[3]),
        pltpu.make_async_copy(wu, wu_v, lsem.at[4]),
    ]
    for q in local:
        q.start()

    rows4 = og[...].astype(F32)
    abuf[r, c, k] = jnp.concatenate(
        [rows4[:, 512 * q : 512 * q + 512] for q in range(4)], axis=0
    ).astype(BF)
    pl.semaphore_wait(barrier, len(offsets) + N + 1)

    sent = []

    def remote(s, d, send, recv, dev):
        return pltpu.make_async_remote_copy(
            src_ref=s, dst_ref=d, send_sem=send, recv_sem=recv, device_id=dev, device_id_type=MESH
        )

    def launch(*args):
        q = remote(*args)
        q.start()
        sent.append(q)

    two = 2 - 4 * c
    near = (two, 1, -1)
    arrivals = (1, -1, 2, -2, 3, -3, 4)
    early = {1: (0, 0, 1), -1: (0, 0, -1), 2: (1, 1, 1), -2: (-1, -1, -1),
             3: (-1, 1, 2), -3: (-1, -1, -2), 4: (2, 2, 2)}
    late = {4: (0, 0, 4), 1: (0, 0, 1), -1: (0, 0, -1), 2: (1, 1, 1), -2: (-1, -1, -1),
            3: (2, 2, 1), -3: (-2, -2, -1)}

    def far_step(buf, sem, tree, m):
        for to, (after, held, step) in tree.items():
            if after == m:
                blk = buf.at[r, c, (k - held + K) % K]
                launch(blk, blk, sem.at[0, to % K], sem.at[1, to % K], chip(NEAR * step))
        blk = buf.at[r, c, (k - m + K) % K]
        for n, d in enumerate(near):
            launch(blk, blk, sem.at[2 + 2 * n, m % K], sem.at[3 + 2 * n, m % K], chip(d))

    def gather(buf, sem, tree):
        for m in arrivals:
            got = buf.at[r, c, (k - m + K) % K]
            remote(got, got, sem.at[0, m % K], sem.at[1, m % K], chip(NEAR)).wait_recv()
            far_step(buf, sem, tree, m)
        group = buf.at[r, c]
        launch(group, group, sem.at[8, 3], sem.at[9, 3], sib)
        for n, d in ((1, 1), (2, -1), (0, two)):
            s = (r - d + NEAR) % NEAR
            for m in (0,) + arrivals:
                got = buf.at[s, c, ((z - d + Z) // NEAR - m + K) % K]
                remote(got, got, sem.at[2 + 2 * n, m % K], sem.at[3 + 2 * n, m % K], chip(d)).wait_recv()
            got = buf.at[s, c]
            launch(got, got, sem.at[8, n], sem.at[9, n], sib)
        for n, d in ((3, 0), (1, 1), (2, -1), (0, 2)):
            got = buf.at[(r - d + NEAR) % NEAR, 1 - c]
            remote(got, got, sem.at[8, n], sem.at[9, n], sib).wait_recv()

    far_step(abuf, a_sem, early, 0)

    o = lax.broadcasted_iota(jnp.int32, (256, 256), 0)
    i = lax.broadcasted_iota(jnp.int32, (256, 256), 1)
    to = ((i // 4) % 4) * 64 + ((i // 16) % 2) * 32 + (i // 64) * 8 + ((i // 32) % 2) * 4 + i % 4
    perm = jnp.where(o == to, 1.0, 0.0).astype(BF)
    rows = Z * 8
    row = lax.broadcasted_iota(jnp.int32, (rows, 2 * rows), 0)
    col = lax.broadcasted_iota(jnp.int32, (rows, 2 * rows), 1)
    src = 8 * (NEAR * ((col // 16) % K) + col // (16 * K)) + col % 8
    half = (col // 8) % 2
    fr_t = frames[...]
    f0 = dot_nn(fr_t, jnp.where((row == src) & (half == 0), 1.0, 0.0).astype(BF)).astype(BF)
    f1 = dot_nn(fr_t, jnp.where((row == src) & (half == 1), 1.0, 0.0).astype(BF)).astype(BF)

    local[1].wait()
    local[2].wait()
    for t in range(N):
        part32 = pl.ds(32 * t, 32)
        gate = gact_v[part32].astype(F32)
        upper = uact_v[part32].astype(F32)
        sigma = jax.nn.sigmoid(gate)
        gate_by[t] = upper * sigma * (1.0 + gate * (1.0 - sigma))
        up_by[t] = gate * sigma
    gather(abuf, a_sem, early)

    for j in range(K // 2):
        rows_in = abuf[:, :, 2 * j : 2 * j + 2].reshape(256, 512)
        out = dot_nn(perm, rows_in).astype(BF)
        for q in range(4):
            full[64 * j : 64 * j + 64, 512 * q : 512 * q + 512] = out[64 * q : 64 * q + 64]
    local[0].wait()
    hpart[...] = dot_nt(full[...], wd_v[...]).reshape(hpart.shape)
    hsend[...] = hpart[...].astype(BF)

    for j in range(1, N):
        launch(hsend.at[(inp + j) % N], hrecv.at[j - 1], hs.at[j], hr.at[j], ring(j))
    total = hpart[inp]
    for j in range(1, N):
        remote(hsend.at[inp], hrecv.at[j - 1], hs.at[j], hr.at[j], ring(j)).wait_recv()
        total = total + hrecv[j - 1].astype(F32)
    hsum[inp] = total.astype(BF)
    for j in range(1, N):
        launch(hsum.at[inp], hsum.at[inp], gs.at[j], gr.at[j], ring(j))

    def grads(t):
        h = hsum[t].astype(F32)
        gu[0, t] = (h * gate_by[t]).astype(BF)
        gu[1, t] = (h * up_by[t]).astype(BF)

    grads(inp)
    local[3].wait()
    local[4].wait()
    for j in range(1, N):
        t = (inp - j + N) % N
        got = hsum.at[t]
        remote(got, got, gs.at[j], gr.at[j], ring(j)).wait_recv()
        grads(t)

    gg = gu[0].reshape(256, 512)
    ug = gu[1].reshape(256, 512)

    def part(start):
        w = pl.ds(pl.multiple_of(start, 512), 512)
        return (dot_nt(gg, wg_v[w, :]) + dot_nt(ug, wu_v[w, :])).reshape(Z, 8, 512)

    for h in range(2):
        sibf[h] = part((1 - c) * 1024 + h * 512)
        launch(sibf.at[h], sibr.at[h], ss.at[h], sr.at[h], sib)
    for h in range(2):
        pown[h] = part(c * 1024 + h * 512)
    for h in range(2):
        remote(sibf.at[h], sibr.at[h], ss.at[h], sr.at[h], sib).wait_recv()
        pown[h] = pown[h] + sibr[h]

    order = sorted(range(K), key=lambda m: -min(m, K - m))
    cut = K // 2

    def rows_of(w):
        w = (w + 2 * Z) % Z
        return jnp.concatenate([pown[0, w], pown[1, w]], axis=0)

    for p in range(2):
        part_m = pl.ds(cut * p, cut)
        for n, d in enumerate(near):
            for t in range(cut * p, cut * p + cut):
                csend[n, t] = rows_of(z + d + NEAR * order[t]).astype(BF)
            launch(csend.at[n, part_m], cnear.at[n, part_m], ns.at[n, p], nr.at[n, p], chip(d))
    for p in range(2):
        part_m = pl.ds(cut * p, cut)
        for n, d in ((1, 1), (2, -1), (0, two)):
            remote(csend.at[n, part_m], cnear.at[n, part_m], ns.at[n, p], nr.at[n, p], chip(d)).wait_recv()
        for t in range(cut * p, cut * p + cut):
            m = order[t]
            total = rows_of(z + NEAR * m)
            for n in range(3):
                total = total + cnear[n, t].astype(F32)
            if m:
                fsend[m] = total.astype(BF)
                launch(fsend.at[m], cfar.at[m], fs.at[m], fr.at[m], chip(NEAR * m))
    for m in sorted(range(1, K), key=lambda m: min(m, K - m)):
        remote(fsend.at[m], cfar.at[m], fs.at[m], fr.at[m], chip(NEAR * m)).wait_recv()
        total = total + cfar[m].astype(F32)
    dbuf[r, c, k] = total.astype(BF)

    far_step(dbuf, d_sem, late, 0)
    gather(dbuf, d_sem, late)

    for a in range(2):
        x = dbuf[:, a].reshape(2 * rows, 512)
        eloc[a, 0:20, 0:512] = dot_nn(f0, x)
        eloc[a, 0:20, 512:1024] = dot_nn(f1, x)
        eloc[a, 20:24, :] = jnp.zeros((4, 1024), F32)
        launch(eloc.at[a], erem.at[a], es.at[a], er.at[a], peer)
    for a in range(2):
        blk = dbuf[r, a, k].astype(F32)
        for h in range(2):
            block8 = blk[8 * h : 8 * h + 8]
            at = 1024 * a + 512 * h
            ig_out[:, at : at + 512] = jnp.where(c == 0, block8[0:4], block8[4:8])
    for a in range(2):
        remote(eloc.at[a], erem.at[a], es.at[a], er.at[a], peer).wait_recv()
        ad_out[:, 1024 * a : 1024 * a + 1024] = eloc[a, 0:20, :] + erem[a, 0:20, :]
    for q in sent:
        q.wait_send()


def finish(ig, ad, ig_out, ad_out):
    ig_out[...] = ig[...].astype(BF)
    ad_out[...] = ad[...]


def per_device(Z, N, out_grad, gate_act, up_act, frames, w_gate, w_up, w_down):
    K = Z // NEAR
    hbm = pl.BlockSpec(memory_space=pl.ANY)
    vmem = pl.BlockSpec(memory_space=pltpu.VMEM)
    dma = pltpu.SemaphoreType.DMA
    ig, ad = pl.pallas_call(
        functools.partial(body, Z, N),
        out_shape=(jax.ShapeDtypeStruct((4, 2048), F32), jax.ShapeDtypeStruct((20, 2048), F32)),
        in_specs=[vmem, hbm, hbm, vmem, hbm, hbm, hbm],
        out_specs=(vmem, vmem),
        scratch_shapes=[
            pltpu.VMEM((NEAR, 2, K, 16, 512), BF),
            pltpu.VMEM((NEAR, 2, K, 16, 512), BF),
            pltpu.VMEM((256, 2048), BF),
            pltpu.VMEM((N, 32, 512), F32),
            pltpu.VMEM((N, 32, 512), BF),
            pltpu.VMEM((N - 1, 32, 512), BF),
            pltpu.VMEM((N, 32, 512), BF),
            pltpu.VMEM((N, 32, 512), F32),
            pltpu.VMEM((N, 32, 512), F32),
            pltpu.VMEM((2, N, 32, 512), BF),
            pltpu.VMEM((256, 512), BF),
            pltpu.VMEM((256, 512), BF),
            pltpu.VMEM((2048, 512), BF),
            pltpu.VMEM((2048, 512), BF),
            pltpu.VMEM((512, 2048), BF),
            pltpu.VMEM((2, Z, 8, 512), F32),
            pltpu.VMEM((2, Z, 8, 512), F32),
            pltpu.VMEM((2, Z, 8, 512), F32),
            pltpu.VMEM((3, K, 16, 512), BF),
            pltpu.VMEM((3, K, 16, 512), BF),
            pltpu.VMEM((K, 16, 512), BF),
            pltpu.VMEM((K, 16, 512), BF),
            pltpu.VMEM((2, 24, 1024), F32),
            pltpu.VMEM((2, 24, 1024), F32),
            dma((5,)),
            dma((10, 8)),
            dma((10, 8)),
            dma((8,)),
            dma((8,)),
            dma((8,)),
            dma((8,)),
            dma((2,)),
            dma((2,)),
            dma((3, 2)),
            dma((3, 2)),
            dma((8,)),
            dma((8,)),
            dma((2,)),
            dma((2,)),
        ],
        compiler_params=pltpu.CompilerParams(
            collective_id=0, has_side_effects=True, vmem_limit_bytes=60 * 1024 * 1024
        ),
        cost_estimate=pl.CostEstimate(flops=1_700_000_000, bytes_accessed=8_000_000, transcendentals=0),
    )(out_grad, gate_act, up_act, frames.T, w_gate, w_up, w_down)
    return pl.pallas_call(
        finish,
        out_shape=(jax.ShapeDtypeStruct((4, 2048), BF), jax.ShapeDtypeStruct((20, 2048), F32)),
        in_specs=[vmem, vmem],
        out_specs=(vmem, vmem),
        compiler_params=pltpu.CompilerParams(vmem_limit_bytes=60 * 1024 * 1024),
    )(ig, ad)


def solution(mesh):
    Z = mesh.shape["hid"] // 2
    N = mesh.shape["inp"]
    return jax.shard_map(
        functools.partial(per_device, Z, N),
        mesh=mesh,
        in_specs=(
            P(("dp", "hid"), "inp"),
            P("dp", "hid"),
            P("dp", "hid"),
            P("dp", "hid"),
            P("inp", "hid"),
            P("inp", "hid"),
            P("hid", "inp"),
        ),
        out_specs=(P(("dp", "hid"), "inp"), P("hid", "inp")),
        check_vma=False,
    )
```

```python
import functools

import jax
import jax.numpy as jnp
from jax import lax
from jax.experimental import pallas as pl
from jax.experimental.pallas import tpu as pltpu
from jax.sharding import PartitionSpec as P

MESH = pl.DeviceIdType.MESH
BF = jnp.bfloat16
F32 = jnp.float32
NEAR = 4


def dot_nt(a, b):
    return lax.dot_general(a, b, (((1,), (1,)), ((), ())), preferred_element_type=F32)


def dot_nn(a, b):
    return lax.dot_general(a, b, (((1,), (0,)), ((), ())), preferred_element_type=F32)


def body(Z, N, *refs):
    (og, gact, uact, frames, wg, wu, wd, ig_out, ad_out,
     abuf, dbuf, full, hpart, hsend, hrecv, hsum, gate_by, up_by, gu, gact_v, uact_v, wg_v, wu_v, wd_v,
     sibf, sibr, pown, csend, cnear, fsend, cfar, eloc, erem,
     lsem, a_sem, d_sem, hs, hr, gs, gr, ss, sr, ns, nr, fs, fr, es, er) = refs
    K = Z // NEAR
    hid = lax.axis_index("hid")
    z = hid // 2
    c = hid % 2
    inp = lax.axis_index("inp")
    dp = lax.axis_index("dp")
    r = z % NEAR
    k = z // NEAR
    sib = {"hid": 2 * z + 1 - c}
    peer = {"dp": 1 - dp}

    def chip(d):
        return {"hid": 2 * ((z + d + 2 * Z) % Z) + c}

    def chip_at(w):
        return {"hid": 2 * w + c}

    def ring(j):
        return {"inp": (inp + j) % N}

    barrier = pltpu.get_barrier_semaphore()
    offsets = (NEAR, Z - NEAR, 1, Z - 1, 2, Z - 2)
    for d in offsets:
        pl.semaphore_signal(barrier, inc=1, device_id=chip(d), device_id_type=MESH)
    for j in range(1, N):
        pl.semaphore_signal(barrier, inc=1, device_id=ring(j), device_id_type=MESH)
    pl.semaphore_signal(barrier, inc=1, device_id=sib, device_id_type=MESH)
    pl.semaphore_signal(barrier, inc=1, device_id=peer, device_id_type=MESH)

    local = [
        pltpu.make_async_copy(wd, wd_v, lsem.at[0]),
        pltpu.make_async_copy(gact, gact_v, lsem.at[1]),
        pltpu.make_async_copy(uact, uact_v, lsem.at[2]),
        pltpu.make_async_copy(wg, wg_v, lsem.at[3]),
        pltpu.make_async_copy(wu, wu_v, lsem.at[4]),
    ]
    for q in local:
        q.start()

    rows4 = og[...].astype(F32)
    abuf[r, c, k] = jnp.concatenate(
        [rows4[:, 512 * q : 512 * q + 512] for q in range(4)], axis=0
    ).astype(BF)
    pl.semaphore_wait(barrier, len(offsets) + N + 1)

    sent = []

    def remote(s, d, send, recv, dev):
        return pltpu.make_async_remote_copy(
            src_ref=s, dst_ref=d, send_sem=send, recv_sem=recv, device_id=dev, device_id_type=MESH
        )

    def launch(*args):
        q = remote(*args)
        q.start()
        sent.append(q)

    two = 2 - 4 * c
    near = (two, 1, -1)
    arrivals = (1, -1, 2, -2, 3, -3, 4)
    early = {1: (0, 0, 1), -1: (0, 0, -1), 2: (1, 1, 1), -2: (-1, -1, -1),
             3: (-1, 1, 2), -3: (-1, -1, -2), 4: (2, 2, 2)}
    late = {4: (0, 0, 4), 1: (0, 0, 1), -1: (0, 0, -1), 2: (1, 1, 1), -2: (-1, -1, -1),
            3: (2, 2, 1), -3: (-2, -2, -1)}

    def far_step(buf, sem, tree, m):
        for to, (after, held, step) in tree.items():
            if after == m:
                blk = buf.at[r, c, (k - held + K) % K]
                launch(blk, blk, sem.at[0, to % K], sem.at[1, to % K], chip(NEAR * step))
        blk = buf.at[r, c, (k - m + K) % K]
        for n, d in enumerate(near):
            launch(blk, blk, sem.at[2 + 2 * n, m % K], sem.at[3 + 2 * n, m % K], chip(d))

    def gather(*chains):
        for m in arrivals:
            for buf, sem, tree in chains:
                got = buf.at[r, c, (k - m + K) % K]
                remote(got, got, sem.at[0, m % K], sem.at[1, m % K], chip(NEAR)).wait_recv()
                far_step(buf, sem, tree, m)
        for buf, sem, tree in chains:
            group = buf.at[r, c]
            launch(group, group, sem.at[8, 3], sem.at[9, 3], sib)
        for n, d in ((1, 1), (2, -1), (0, two)):
            s = (r - d + NEAR) % NEAR
            for buf, sem, tree in chains:
                for m in (0,) + arrivals:
                    got = buf.at[s, c, ((z - d + Z) // NEAR - m + K) % K]
                    remote(got, got, sem.at[2 + 2 * n, m % K], sem.at[3 + 2 * n, m % K], chip(d)).wait_recv()
                got = buf.at[s, c]
                launch(got, got, sem.at[8, n], sem.at[9, n], sib)

    def from_other_core(buf, sem):
        for n, d in ((3, 0), (1, 1), (2, -1), (0, 2)):
            got = buf.at[(r - d + NEAR) % NEAR, 1 - c]
            remote(got, got, sem.at[8, n], sem.at[9, n], sib).wait_recv()

    far_step(abuf, a_sem, early, 0)

    o = lax.broadcasted_iota(jnp.int32, (256, 256), 0)
    i = lax.broadcasted_iota(jnp.int32, (256, 256), 1)
    to = ((i // 4) % 4) * 64 + ((i // 16) % 2) * 32 + (i // 64) * 8 + ((i // 32) % 2) * 4 + i % 4
    perm = jnp.where(o == to, 1.0, 0.0).astype(BF)
    rows = Z * 8
    row = lax.broadcasted_iota(jnp.int32, (rows, 2 * rows), 0)
    col = lax.broadcasted_iota(jnp.int32, (rows, 2 * rows), 1)
    src = 8 * (NEAR * ((col // 16) % K) + col // (16 * K)) + col % 8
    half = (col // 8) % 2
    fr_t = frames[...]
    f0 = dot_nn(fr_t, jnp.where((row == src) & (half == 0), 1.0, 0.0).astype(BF)).astype(BF)
    f1 = dot_nn(fr_t, jnp.where((row == src) & (half == 1), 1.0, 0.0).astype(BF)).astype(BF)

    local[1].wait()
    local[2].wait()
    for t in range(N):
        part32 = pl.ds(32 * t, 32)
        gate = gact_v[part32].astype(F32)
        upper = uact_v[part32].astype(F32)
        sigma = jax.nn.sigmoid(gate)
        gate_by[t] = upper * sigma * (1.0 + gate * (1.0 - sigma))
        up_by[t] = gate * sigma
    gather((abuf, a_sem, early))
    from_other_core(abuf, a_sem)

    for j in range(K // 2):
        rows_in = abuf[:, :, 2 * j : 2 * j + 2].reshape(256, 512)
        out = dot_nn(perm, rows_in).astype(BF)
        for q in range(4):
            full[64 * j : 64 * j + 64, 512 * q : 512 * q + 512] = out[64 * q : 64 * q + 64]
    local[0].wait()
    hpart[...] = dot_nt(full[...], wd_v[...]).reshape(hpart.shape)
    hsend[...] = hpart[...].astype(BF)

    for j in range(1, N):
        launch(hsend.at[(inp + j) % N], hrecv.at[j - 1], hs.at[j], hr.at[j], ring(j))
    total = hpart[inp]
    for j in range(1, N):
        remote(hsend.at[inp], hrecv.at[j - 1], hs.at[j], hr.at[j], ring(j)).wait_recv()
        total = total + hrecv[j - 1].astype(F32)
    hsum[inp] = total.astype(BF)
    for j in range(1, N):
        launch(hsum.at[inp], hsum.at[inp], gs.at[j], gr.at[j], ring(j))

    def grads(t):
        h = hsum[t].astype(F32)
        gu[0, t] = (h * gate_by[t]).astype(BF)
        gu[1, t] = (h * up_by[t]).astype(BF)

    grads(inp)
    local[3].wait()
    local[4].wait()
    for j in range(1, N):
        t = (inp - j + N) % N
        got = hsum.at[t]
        remote(got, got, gs.at[j], gr.at[j], ring(j)).wait_recv()
        grads(t)

    gg = gu[0].reshape(256, 512)
    ug = gu[1].reshape(256, 512)

    def part(start):
        w = pl.ds(pl.multiple_of(start, 512), 512)
        return (dot_nt(gg, wg_v[w, :]) + dot_nt(ug, wu_v[w, :])).reshape(Z, 8, 512)

    order = sorted(range(K), key=lambda m: -min(m, K - m))

    def rows_of(h, w):
        own = pown[h, (w + 2 * Z) % Z]
        return jnp.concatenate([own[:, 0:256], own[:, 256:512]], axis=0)

    for h in range(2):
        sibf[h] = part((1 - c) * 1024 + h * 512)
        launch(sibf.at[h], sibr.at[h], ss.at[h], sr.at[h], sib)
        pown[h] = part(c * 1024 + h * 512)
        remote(sibf.at[h], sibr.at[h], ss.at[h], sr.at[h], sib).wait_recv()
        pown[h] = pown[h] + sibr[h]
        for n, d in enumerate(near):
            for t in range(K):
                csend[h, n, t] = rows_of(h, z + d + NEAR * order[t]).astype(BF)
            launch(csend.at[h, n], cnear.at[h, n], ns.at[h, n], nr.at[h, n], chip(d))
    last = [None, None]
    for h in range(2):
        for n, d in ((1, 1), (2, -1), (0, two)):
            remote(csend.at[h, n], cnear.at[h, n], ns.at[h, n], nr.at[h, n], chip(d)).wait_recv()
        for t in range(K):
            m = order[t]
            total = rows_of(h, z + NEAR * m)
            for n in range(3):
                total = total + cnear[h, n, t].astype(F32)
            if m:
                fsend[h, m] = total.astype(BF)
                launch(fsend.at[h, m], cfar.at[h, m], fs.at[h, m], fr.at[h, m], chip(NEAR * m))
        last[h] = total
    for h in range(2):
        total = last[h]
        for m in sorted(range(1, K), key=lambda m: min(m, K - m)):
            remote(fsend.at[h, m], cfar.at[h, m], fs.at[h, m], fr.at[h, m], chip(NEAR * m)).wait_recv()
            total = total + cfar[h, m].astype(F32)
        dbuf[h, r, c, k] = total.astype(BF)
        far_step(dbuf.at[h], d_sem.at[h], late, 0)

    gather(*((dbuf.at[h], d_sem.at[h], late) for h in range(2)))

    for h in range(2):
        from_other_core(dbuf.at[h], d_sem.at[h])
        for a in range(2):
            x = dbuf[h, :, a].reshape(2 * rows, 256)
            eloc[h, 0:20, 512 * a : 512 * a + 256] = dot_nn(f0, x)
            eloc[h, 0:20, 512 * a + 256 : 512 * a + 512] = dot_nn(f1, x)
        eloc[h, 20:24, :] = jnp.zeros((4, 1024), F32)
        launch(eloc.at[h], erem.at[h], es.at[h], er.at[h], peer)
    for h in range(2):
        for a in range(2):
            blk = dbuf[h, r, a, k].astype(F32)
            for e in range(2):
                block8 = blk[8 * e : 8 * e + 8]
                at = 1024 * a + 512 * h + 256 * e
                ig_out[:, at : at + 256] = jnp.where(c == 0, block8[0:4], block8[4:8])
    for h in range(2):
        remote(eloc.at[h], erem.at[h], es.at[h], er.at[h], peer).wait_recv()
        for a in range(2):
            at = 1024 * a + 512 * h
            cols = pl.ds(512 * a, 512)
            ad_out[:, at : at + 512] = eloc[h, 0:20, cols] + erem[h, 0:20, cols]
    for q in sent:
        q.wait_send()


def finish(ig, ad, ig_out, ad_out):
    ig_out[...] = ig[...].astype(BF)
    ad_out[...] = ad[...]


def per_device(Z, N, out_grad, gate_act, up_act, frames, w_gate, w_up, w_down):
    K = Z // NEAR
    hbm = pl.BlockSpec(memory_space=pl.ANY)
    vmem = pl.BlockSpec(memory_space=pltpu.VMEM)
    dma = pltpu.SemaphoreType.DMA
    ig, ad = pl.pallas_call(
        functools.partial(body, Z, N),
        out_shape=(jax.ShapeDtypeStruct((4, 2048), F32), jax.ShapeDtypeStruct((20, 2048), F32)),
        in_specs=[vmem, hbm, hbm, vmem, hbm, hbm, hbm],
        out_specs=(vmem, vmem),
        scratch_shapes=[
            pltpu.VMEM((NEAR, 2, K, 16, 512), BF),
            pltpu.VMEM((2, NEAR, 2, K, 16, 256), BF),
            pltpu.VMEM((256, 2048), BF),
            pltpu.VMEM((N, 32, 512), F32),
            pltpu.VMEM((N, 32, 512), BF),
            pltpu.VMEM((N - 1, 32, 512), BF),
            pltpu.VMEM((N, 32, 512), BF),
            pltpu.VMEM((N, 32, 512), F32),
            pltpu.VMEM((N, 32, 512), F32),
            pltpu.VMEM((2, N, 32, 512), BF),
            pltpu.VMEM((256, 512), BF),
            pltpu.VMEM((256, 512), BF),
            pltpu.VMEM((2048, 512), BF),
            pltpu.VMEM((2048, 512), BF),
            pltpu.VMEM((512, 2048), BF),
            pltpu.VMEM((2, Z, 8, 512), F32),
            pltpu.VMEM((2, Z, 8, 512), F32),
            pltpu.VMEM((2, Z, 8, 512), F32),
            pltpu.VMEM((2, 3, K, 16, 256), BF),
            pltpu.VMEM((2, 3, K, 16, 256), BF),
            pltpu.VMEM((2, K, 16, 256), BF),
            pltpu.VMEM((2, K, 16, 256), BF),
            pltpu.VMEM((2, 24, 1024), F32),
            pltpu.VMEM((2, 24, 1024), F32),
            dma((5,)),
            dma((10, 8)),
            dma((2, 10, 8)),
            dma((8,)),
            dma((8,)),
            dma((8,)),
            dma((8,)),
            dma((2,)),
            dma((2,)),
            dma((2, 3)),
            dma((2, 3)),
            dma((2, 8)),
            dma((2, 8)),
            dma((2,)),
            dma((2,)),
        ],
        compiler_params=pltpu.CompilerParams(
            collective_id=0, has_side_effects=True, vmem_limit_bytes=60 * 1024 * 1024
        ),
        cost_estimate=pl.CostEstimate(flops=1_700_000_000, bytes_accessed=8_000_000, transcendentals=0),
    )(out_grad, gate_act, up_act, frames.T, w_gate, w_up, w_down)
    return pl.pallas_call(
        finish,
        out_shape=(jax.ShapeDtypeStruct((4, 2048), BF), jax.ShapeDtypeStruct((20, 2048), F32)),
        in_specs=[vmem, vmem],
        out_specs=(vmem, vmem),
        compiler_params=pltpu.CompilerParams(vmem_limit_bytes=60 * 1024 * 1024),
    )(ig, ad)


def solution(mesh):
    Z = mesh.shape["hid"] // 2
    N = mesh.shape["inp"]
    return jax.shard_map(
        functools.partial(per_device, Z, N),
        mesh=mesh,
        in_specs=(
            P(("dp", "hid"), "inp"),
            P("dp", "hid"),
            P("dp", "hid"),
            P("dp", "hid"),
            P("inp", "hid"),
            P("inp", "hid"),
            P("hid", "inp"),
        ),
        out_specs=(P(("dp", "hid"), "inp"), P("hid", "inp")),
        check_vma=False,
    )
```

```python
import functools

import jax
import jax.numpy as jnp
from jax import lax
from jax.experimental import pallas as pl
from jax.experimental.pallas import tpu as pltpu
from jax.sharding import PartitionSpec as P

MESH = pl.DeviceIdType.MESH
BF = jnp.bfloat16
F32 = jnp.float32
NEAR = 4


def dot_nt(a, b):
    return lax.dot_general(a, b, (((1,), (1,)), ((), ())), preferred_element_type=F32)


def dot_nn(a, b):
    return lax.dot_general(a, b, (((1,), (0,)), ((), ())), preferred_element_type=F32)


def body(Z, N, *refs):
    (og, gact, uact, frames, wg, wu, wd, ig_out, ad_out,
     abuf, dbuf, full, hpart, hsend, hrecv, hsum, gate_by, up_by, gu, gact_v, uact_v, wg_v, wu_v, wd_v,
     sibf, sibr, pown, csend, cnear, fsend, cfar, eloc, erem,
     lsem, a_sem, d_sem, hs, hr, gs, gr, ss, sr, ns, nr, fs, fr, es, er) = refs
    K = Z // NEAR
    hid = lax.axis_index("hid")
    z = hid // 2
    c = hid % 2
    inp = lax.axis_index("inp")
    dp = lax.axis_index("dp")
    r = z % NEAR
    k = z // NEAR
    sib = {"hid": 2 * z + 1 - c}
    peer = {"dp": 1 - dp}

    def chip(d):
        return {"hid": 2 * ((z + d + 2 * Z) % Z) + c}

    def chip_at(w):
        return {"hid": 2 * w + c}

    def ring(j):
        return {"inp": (inp + j) % N}

    barrier = pltpu.get_barrier_semaphore()
    offsets = (NEAR, Z - NEAR, 1, Z - 1, 2, Z - 2)
    for d in offsets:
        pl.semaphore_signal(barrier, inc=1, device_id=chip(d), device_id_type=MESH)
    for j in range(1, N):
        pl.semaphore_signal(barrier, inc=1, device_id=ring(j), device_id_type=MESH)
    pl.semaphore_signal(barrier, inc=1, device_id=sib, device_id_type=MESH)
    pl.semaphore_signal(barrier, inc=1, device_id=peer, device_id_type=MESH)

    local = [
        pltpu.make_async_copy(wd, wd_v, lsem.at[0]),
        pltpu.make_async_copy(gact, gact_v, lsem.at[1]),
        pltpu.make_async_copy(uact, uact_v, lsem.at[2]),
        pltpu.make_async_copy(wg, wg_v, lsem.at[3]),
        pltpu.make_async_copy(wu, wu_v, lsem.at[4]),
    ]
    for q in local:
        q.start()

    rows4 = og[...].astype(F32)
    abuf[r, c, k] = jnp.concatenate(
        [rows4[:, 512 * q : 512 * q + 512] for q in range(4)], axis=0
    ).astype(BF)
    pl.semaphore_wait(barrier, len(offsets) + N + 1)

    def remote(s, d, send, recv, dev):
        return pltpu.make_async_remote_copy(
            src_ref=s, dst_ref=d, send_sem=send, recv_sem=recv, device_id=dev, device_id_type=MESH
        )

    def launch(*args):
        remote(*args).start()

    def wait_sent(ref, sem):
        remote(ref, ref, sem, sem, sib).wait_send()

    def wait_received(ref, sem):
        remote(ref, ref, sem, sem, sib).wait_recv()

    two = 2 - 4 * c
    near = (two, 1, -1)
    arrivals = (1, -1, 2, -2, 3, -3, 4)
    early = {1: (0, 0, 1), -1: (0, 0, -1), 2: (1, 1, 1), -2: (-1, -1, -1),
             3: (-1, 1, 2), -3: (-1, -1, -2), 4: (2, 2, 2)}
    late = {4: (0, 0, 4), 1: (0, 0, 1), -1: (0, 0, -1), 2: (1, 1, 1), -2: (-1, -1, -1),
            3: (2, 2, 1), -3: (-2, -2, -1)}

    def far_step(buf, sem, tree, m):
        for to, (after, held, step) in tree.items():
            if after == m:
                blk = buf.at[r, c, (k - held + K) % K]
                launch(blk, blk, sem.at[0], sem.at[10 + to % K], chip(NEAR * step))
        blk = buf.at[r, c, (k - m + K) % K]
        for n, d in enumerate(near):
            launch(blk, blk, sem.at[1], sem.at[3 + n], chip(d))

    def gather(buf, sem, tree):
        for m in arrivals:
            wait_received(buf.at[r, c, (k - m + K) % K], sem.at[10 + m % K])
            far_step(buf, sem, tree, m)
        group = buf.at[r, c]
        launch(group, group, sem.at[2], sem.at[9], sib)
        for n, d in ((1, 1), (2, -1), (0, two)):
            got = buf.at[(r - d + NEAR) % NEAR, c]
            wait_received(got, sem.at[3 + n])
            launch(got, got, sem.at[2], sem.at[6 + n], sib)

    def from_other_core(buf, sem):
        for n, d in ((3, 0), (1, 1), (2, -1), (0, 2)):
            wait_received(buf.at[(r - d + NEAR) % NEAR, 1 - c], sem.at[6 + n])

    def gather_sent(buf, sem):
        wait_sent(buf.at[0, 0, pl.ds(0, K - 1)], sem.at[0])
        wait_sent(buf.at[pl.ds(0, 3), 0], sem.at[1])

    far_step(abuf, a_sem, early, 0)

    o = lax.broadcasted_iota(jnp.int32, (256, 256), 0)
    i = lax.broadcasted_iota(jnp.int32, (256, 256), 1)
    to = ((i // 4) % 4) * 64 + ((i // 16) % 2) * 32 + (i // 64) * 8 + ((i // 32) % 2) * 4 + i % 4
    perm = jnp.where(o == to, 1.0, 0.0).astype(BF)
    rows = Z * 8
    row = lax.broadcasted_iota(jnp.int32, (rows, 2 * rows), 0)
    col = lax.broadcasted_iota(jnp.int32, (rows, 2 * rows), 1)
    src = 8 * (NEAR * ((col // 16) % K) + col // (16 * K)) + col % 8
    half = (col // 8) % 2
    fr_t = frames[...]
    f0 = dot_nn(fr_t, jnp.where((row == src) & (half == 0), 1.0, 0.0).astype(BF)).astype(BF)
    f1 = dot_nn(fr_t, jnp.where((row == src) & (half == 1), 1.0, 0.0).astype(BF)).astype(BF)

    local[1].wait()
    local[2].wait()
    for t in range(N):
        part32 = pl.ds(32 * t, 32)
        gate = gact_v[part32].astype(F32)
        upper = uact_v[part32].astype(F32)
        sigma = jax.nn.sigmoid(gate)
        gate_by[t] = upper * sigma * (1.0 + gate * (1.0 - sigma))
        up_by[t] = gate * sigma
    gather(abuf, a_sem, early)
    from_other_core(abuf, a_sem)

    for j in range(K // 2):
        rows_in = abuf[:, :, 2 * j : 2 * j + 2].reshape(256, 512)
        out = dot_nn(perm, rows_in).astype(BF)
        for q in range(4):
            full[64 * j : 64 * j + 64, 512 * q : 512 * q + 512] = out[64 * q : 64 * q + 64]
    local[0].wait()
    hpart[...] = dot_nt(full[...], wd_v[...]).reshape(hpart.shape)
    hsend[...] = hpart[...].astype(BF)

    for j in range(1, N):
        launch(hsend.at[(inp + j) % N], hrecv.at[j - 1], hs, hr, ring(j))
    total = hpart[inp]
    wait_received(hrecv, hr)
    for j in range(1, N):
        total = total + hrecv[j - 1].astype(F32)
    hsum[inp] = total.astype(BF)
    for j in range(1, N):
        launch(hsum.at[inp], hsum.at[inp], gs, gr, ring(j))

    def grads(t):
        h = hsum[t].astype(F32)
        gu[0, t] = (h * gate_by[t]).astype(BF)
        gu[1, t] = (h * up_by[t]).astype(BF)

    grads(inp)
    local[3].wait()
    local[4].wait()
    wait_received(hsum.at[pl.ds(0, N - 1)], gr)
    for j in range(1, N):
        grads((inp - j + N) % N)

    gg = gu[0].reshape(256, 512)
    ug = gu[1].reshape(256, 512)

    def part(start):
        w = pl.ds(pl.multiple_of(start, 512), 512)
        return (dot_nt(gg, wg_v[w, :]) + dot_nt(ug, wu_v[w, :])).reshape(Z, 8, 512)

    for h in range(2):
        sibf[h] = part((1 - c) * 1024 + h * 512)
        launch(sibf.at[h], sibr.at[h], ss, sr.at[h], sib)
    for h in range(2):
        pown[h] = part(c * 1024 + h * 512)
    for h in range(2):
        wait_received(sibr.at[h], sr.at[h])
        pown[h] = pown[h] + sibr[h]

    order = sorted(range(K), key=lambda m: -min(m, K - m))
    cut = K // 2

    def rows_of(w):
        w = (w + 2 * Z) % Z
        return jnp.concatenate([pown[0, w], pown[1, w]], axis=0)

    for p in range(2):
        part_m = pl.ds(cut * p, cut)
        for n, d in enumerate(near):
            for t in range(cut * p, cut * p + cut):
                csend[n, t] = rows_of(z + d + NEAR * order[t]).astype(BF)
            launch(csend.at[n, part_m], cnear.at[n, part_m], ns, nr.at[n, p], chip(d))
    for p in range(2):
        part_m = pl.ds(cut * p, cut)
        for n, d in ((1, 1), (2, -1), (0, two)):
            wait_received(cnear.at[n, part_m], nr.at[n, p])
        for t in range(cut * p, cut * p + cut):
            m = order[t]
            total = rows_of(z + NEAR * m)
            for n in range(3):
                total = total + cnear[n, t].astype(F32)
            if m:
                fsend[m] = total.astype(BF)
                launch(fsend.at[m], cfar.at[m], fs, fr, chip(NEAR * m))
    others = pl.ds(1, K - 1)
    wait_received(cfar.at[others], fr)
    for m in range(1, K):
        total = total + cfar[m].astype(F32)
    dbuf[r, c, k] = total.astype(BF)

    far_step(dbuf, d_sem, late, 0)
    gather_sent(abuf, a_sem)
    wait_sent(abuf.at[:, 0], a_sem.at[2])
    wait_sent(hsend.at[pl.ds(0, N - 1)], hs)
    wait_sent(hsum.at[pl.ds(0, N - 1)], gs)
    wait_sent(sibf, ss)
    wait_sent(csend, ns)
    wait_sent(fsend.at[others], fs)
    gather(dbuf, d_sem, late)

    def adapter_part(a):
        x = dbuf[:, a].reshape(2 * rows, 512)
        eloc[a, 0:20, 0:512] = dot_nn(f0, x)
        eloc[a, 0:20, 512:1024] = dot_nn(f1, x)
        launch(eloc.at[a], erem.at[a], es, er.at[a], peer)

    eloc[:, 20:24, :] = jnp.zeros((2, 4, 1024), F32)
    adapter_part(c)
    gather_sent(dbuf, d_sem)
    from_other_core(dbuf, d_sem)
    adapter_part(1 - c)
    for a in range(2):
        blk = dbuf[r, a, k].astype(F32)
        for h in range(2):
            block8 = blk[8 * h : 8 * h + 8]
            at = 1024 * a + 512 * h
            ig_out[:, at : at + 512] = jnp.where(c == 0, block8[0:4], block8[4:8])
    wait_sent(dbuf.at[:, 0], d_sem.at[2])
    for a in range(2):
        wait_received(erem.at[a], er.at[a])
        ad_out[:, 1024 * a : 1024 * a + 1024] = eloc[a, 0:20, :] + erem[a, 0:20, :]
    wait_sent(eloc, es)


def finish(ig, ad, ig_out, ad_out):
    ig_out[...] = ig[...].astype(BF)
    ad_out[...] = ad[...]


def per_device(Z, N, out_grad, gate_act, up_act, frames, w_gate, w_up, w_down):
    K = Z // NEAR
    hbm = pl.BlockSpec(memory_space=pl.ANY)
    vmem = pl.BlockSpec(memory_space=pltpu.VMEM)
    dma = pltpu.SemaphoreType.DMA
    ig, ad = pl.pallas_call(
        functools.partial(body, Z, N),
        out_shape=(jax.ShapeDtypeStruct((4, 2048), F32), jax.ShapeDtypeStruct((20, 2048), F32)),
        in_specs=[vmem, hbm, hbm, vmem, hbm, hbm, hbm],
        out_specs=(vmem, vmem),
        scratch_shapes=[
            pltpu.VMEM((NEAR, 2, K, 16, 512), BF),
            pltpu.VMEM((NEAR, 2, K, 16, 512), BF),
            pltpu.VMEM((256, 2048), BF),
            pltpu.VMEM((N, 32, 512), F32),
            pltpu.VMEM((N, 32, 512), BF),
            pltpu.VMEM((N - 1, 32, 512), BF),
            pltpu.VMEM((N, 32, 512), BF),
            pltpu.VMEM((N, 32, 512), F32),
            pltpu.VMEM((N, 32, 512), F32),
            pltpu.VMEM((2, N, 32, 512), BF),
            pltpu.VMEM((256, 512), BF),
            pltpu.VMEM((256, 512), BF),
            pltpu.VMEM((2048, 512), BF),
            pltpu.VMEM((2048, 512), BF),
            pltpu.VMEM((512, 2048), BF),
            pltpu.VMEM((2, Z, 8, 512), F32),
            pltpu.VMEM((2, Z, 8, 512), F32),
            pltpu.VMEM((2, Z, 8, 512), F32),
            pltpu.VMEM((3, K, 16, 512), BF),
            pltpu.VMEM((3, K, 16, 512), BF),
            pltpu.VMEM((K, 16, 512), BF),
            pltpu.VMEM((K, 16, 512), BF),
            pltpu.VMEM((2, 24, 1024), F32),
            pltpu.VMEM((2, 24, 1024), F32),
            dma((5,)),
            dma((18,)),
            dma((18,)),
            dma,
            dma,
            dma,
            dma,
            dma,
            dma((2,)),
            dma,
            dma((3, 2)),
            dma,
            dma,
            dma,
            dma((2,)),
        ],
        compiler_params=pltpu.CompilerParams(
            collective_id=0, has_side_effects=True, vmem_limit_bytes=60 * 1024 * 1024
        ),
        cost_estimate=pl.CostEstimate(flops=1_700_000_000, bytes_accessed=8_000_000, transcendentals=0),
    )(out_grad, gate_act, up_act, frames.T, w_gate, w_up, w_down)
    return pl.pallas_call(
        finish,
        out_shape=(jax.ShapeDtypeStruct((4, 2048), BF), jax.ShapeDtypeStruct((20, 2048), F32)),
        in_specs=[vmem, vmem],
        out_specs=(vmem, vmem),
        compiler_params=pltpu.CompilerParams(vmem_limit_bytes=60 * 1024 * 1024),
    )(ig, ad)


def solution(mesh):
    Z = mesh.shape["hid"] // 2
    N = mesh.shape["inp"]
    return jax.shard_map(
        functools.partial(per_device, Z, N),
        mesh=mesh,
        in_specs=(
            P(("dp", "hid"), "inp"),
            P("dp", "hid"),
            P("dp", "hid"),
            P("dp", "hid"),
            P("inp", "hid"),
            P("inp", "hid"),
            P("hid", "inp"),
        ),
        out_specs=(P(("dp", "hid"), "inp"), P("hid", "inp")),
        check_vma=False,
    )
```

```python
import functools

import jax
import jax.numpy as jnp
from jax import lax
from jax.experimental import pallas as pl
from jax.experimental.pallas import tpu as pltpu
from jax.sharding import PartitionSpec as P

MESH = pl.DeviceIdType.MESH
BF = jnp.bfloat16
F32 = jnp.float32
NEAR = 4


def dot_nt(a, b):
    return lax.dot_general(a, b, (((1,), (1,)), ((), ())), preferred_element_type=F32)


def dot_nn(a, b):
    return lax.dot_general(a, b, (((1,), (0,)), ((), ())), preferred_element_type=F32)


def body(Z, N, *refs):
    (og, gact, uact, frames, wg, wu, wd, ig_out, ad_out,
     abuf, dbuf, full, hpart, hsend, hrecv, hsum, gate_by, up_by, gu, gact_v, uact_v, wg_v, wu_v, wd_v,
     sibf, sibr, pown, csend, cnear, fsend, cfar, eloc, erem,
     lsem, a_sem, d_sem, hs, hr, gs, gr, ss, sr, ns, nr, fs, fr, es, er) = refs
    K = Z // NEAR
    hid = lax.axis_index("hid")
    z = hid // 2
    c = hid % 2
    inp = lax.axis_index("inp")
    dp = lax.axis_index("dp")
    r = z % NEAR
    k = z // NEAR
    sib = {"hid": 2 * z + 1 - c}
    peer = {"dp": 1 - dp}

    def chip(d):
        return {"hid": 2 * ((z + d + 2 * Z) % Z) + c}

    def chip_at(w):
        return {"hid": 2 * w + c}

    def ring(j):
        return {"inp": (inp + j) % N}

    barrier = pltpu.get_barrier_semaphore()
    offsets = (NEAR, Z - NEAR, 1, Z - 1, 2, Z - 2)
    for d in offsets:
        pl.semaphore_signal(barrier, inc=1, device_id=chip(d), device_id_type=MESH)
    for j in range(1, N):
        pl.semaphore_signal(barrier, inc=1, device_id=ring(j), device_id_type=MESH)
    pl.semaphore_signal(barrier, inc=1, device_id=sib, device_id_type=MESH)
    pl.semaphore_signal(barrier, inc=1, device_id=peer, device_id_type=MESH)

    local = [
        pltpu.make_async_copy(wd, wd_v, lsem.at[0]),
        pltpu.make_async_copy(gact, gact_v, lsem.at[1]),
        pltpu.make_async_copy(uact, uact_v, lsem.at[2]),
        pltpu.make_async_copy(wg, wg_v, lsem.at[3]),
        pltpu.make_async_copy(wu, wu_v, lsem.at[4]),
    ]
    for q in local:
        q.start()

    rows4 = og[...].astype(F32)
    abuf[r, c, k] = jnp.concatenate(
        [rows4[:, 512 * q : 512 * q + 512] for q in range(4)], axis=0
    ).astype(BF)
    pl.semaphore_wait(barrier, len(offsets) + N + 1)

    def remote(s, d, send, recv, dev):
        return pltpu.make_async_remote_copy(
            src_ref=s, dst_ref=d, send_sem=send, recv_sem=recv, device_id=dev, device_id_type=MESH
        )

    def launch(*args):
        remote(*args).start()

    def wait_sent(ref, sem):
        remote(ref, ref, sem, sem, sib).wait_send()

    def wait_received(ref, sem):
        remote(ref, ref, sem, sem, sib).wait_recv()

    two = 2 - 4 * c
    near = (two, 1, -1)
    arrivals = ((1, -1), (2, -2), (3, -3, 4))
    early = {1: (0, 0, 1), -1: (0, 0, -1), 2: (1, 1, 1), -2: (-1, -1, -1),
             3: (-1, 1, 2), -3: (-1, -1, -2), 4: (2, 2, 2)}
    late = {4: (0, 0, 4), 1: (0, 0, 1), -1: (0, 0, -1), 2: (1, 1, 1), -2: (-1, -1, -1),
            3: (2, 2, 1), -3: (-2, -2, -1)}

    def far_step(buf, sem, tree, m, whole=False):
        for to, (after, held, step) in tree.items():
            if after == m:
                blk = buf.at[r, c, (k - held + K) % K]
                launch(blk, blk, sem.at[0], sem.at[10 + to % K], chip(NEAR * step))
        if not whole:
            near_step(buf.at[r, c, (k - m + K) % K], sem)

    def near_step(blk, sem):
        for n, d in enumerate(near):
            launch(blk, blk, sem.at[1], sem.at[3 + n], chip(d))

    def far_gather(*chains):
        for wave in arrivals:
            for buf, sem, tree, whole in chains:
                for m in wave:
                    wait_received(buf.at[r, c, (k - m + K) % K], sem.at[10 + m % K])
                    far_step(buf, sem, tree, m, whole)
                if wave is arrivals[-1]:
                    group = buf.at[r, c]
                    if whole:
                        near_step(group, sem)
                    launch(group, group, sem.at[2], sem.at[9], sib)

    def near_gather(buf, sem):
        for n, d in ((1, 1), (2, -1), (0, two)):
            got = buf.at[(r - d + NEAR) % NEAR, c]
            wait_received(got, sem.at[3 + n])
            launch(got, got, sem.at[2], sem.at[6 + n], sib)

    def from_other_core(buf, sem):
        for n, d in ((3, 0), (1, 1), (2, -1), (0, 2)):
            wait_received(buf.at[(r - d + NEAR) % NEAR, 1 - c], sem.at[6 + n])

    def gather_sent(buf, sem):
        wait_sent(buf.at[0, 0, pl.ds(0, K - 1)], sem.at[0])
        wait_sent(buf.at[pl.ds(0, 3), 0], sem.at[1])

    far_step(abuf, a_sem, early, 0)

    o = lax.broadcasted_iota(jnp.int32, (256, 256), 0)
    i = lax.broadcasted_iota(jnp.int32, (256, 256), 1)
    to = ((i // 4) % 4) * 64 + ((i // 16) % 2) * 32 + (i // 64) * 8 + ((i // 32) % 2) * 4 + i % 4
    perm = jnp.where(o == to, 1.0, 0.0).astype(BF)
    rows = Z * 8
    row = lax.broadcasted_iota(jnp.int32, (rows, 2 * rows), 0)
    col = lax.broadcasted_iota(jnp.int32, (rows, 2 * rows), 1)
    src = 8 * (NEAR * ((col // 16) % K) + col // (16 * K)) + col % 8
    half = (col // 8) % 2
    fr_t = frames[...]
    f0 = dot_nn(fr_t, jnp.where((row == src) & (half == 0), 1.0, 0.0).astype(BF)).astype(BF)
    f1 = dot_nn(fr_t, jnp.where((row == src) & (half == 1), 1.0, 0.0).astype(BF)).astype(BF)

    local[1].wait()
    local[2].wait()
    for t in range(N):
        part32 = pl.ds(32 * t, 32)
        gate = gact_v[part32].astype(F32)
        upper = uact_v[part32].astype(F32)
        sigma = jax.nn.sigmoid(gate)
        gate_by[t] = upper * sigma * (1.0 + gate * (1.0 - sigma))
        up_by[t] = gate * sigma
    far_gather((abuf, a_sem, early, False))
    near_gather(abuf, a_sem)
    from_other_core(abuf, a_sem)

    for j in range(K // 2):
        rows_in = abuf[:, :, 2 * j : 2 * j + 2].reshape(256, 512)
        out = dot_nn(perm, rows_in).astype(BF)
        for q in range(4):
            full[64 * j : 64 * j + 64, 512 * q : 512 * q + 512] = out[64 * q : 64 * q + 64]
    local[0].wait()
    hpart[...] = dot_nt(full[...], wd_v[...]).reshape(hpart.shape)
    hsend[...] = hpart[...].astype(BF)

    for j in range(1, N):
        launch(hsend.at[(inp + j) % N], hrecv.at[j - 1], hs, hr, ring(j))
    total = hpart[inp]
    wait_received(hrecv, hr)
    for j in range(1, N):
        total = total + hrecv[j - 1].astype(F32)
    hsum[inp] = total.astype(BF)
    for j in range(1, N):
        launch(hsum.at[inp], hsum.at[inp], gs, gr, ring(j))

    def grads(t):
        h = hsum[t].astype(F32)
        gu[0, t] = (h * gate_by[t]).astype(BF)
        gu[1, t] = (h * up_by[t]).astype(BF)

    grads(inp)
    local[3].wait()
    local[4].wait()
    wait_received(hsum.at[pl.ds(0, N - 1)], gr)
    for j in range(1, N):
        grads((inp - j + N) % N)

    gg = gu[0].reshape(256, 512)
    ug = gu[1].reshape(256, 512)

    def part(start):
        w = pl.ds(pl.multiple_of(start, 512), 512)
        return (dot_nt(gg, wg_v[w, :]) + dot_nt(ug, wu_v[w, :])).reshape(Z, 8, 512)

    order = sorted(range(K), key=lambda m: -min(m, K - m))

    def rows_of(h, w):
        own = pown[h, (w + 2 * Z) % Z]
        return jnp.concatenate([own[:, 0:256], own[:, 256:512]], axis=0)

    for h in range(2):
        sibf[h] = part((1 - c) * 1024 + h * 512)
        launch(sibf.at[h], sibr.at[h], ss, sr.at[h], sib)
        pown[h] = part(c * 1024 + h * 512)
        wait_received(sibr.at[h], sr.at[h])
        pown[h] = pown[h] + sibr[h]
        for n, d in enumerate(near):
            for t in range(K):
                csend[h, n, t] = rows_of(h, z + d + NEAR * order[t]).astype(BF)
            launch(csend.at[h, n], cnear.at[h, n], ns, nr.at[h, n], chip(d))
    others = pl.ds(1, K - 1)
    last = [None, None]
    for h in range(2):
        for n in (1, 2, 0):
            wait_received(cnear.at[h, n], nr.at[h, n])
        for t in range(K):
            m = order[t]
            total = rows_of(h, z + NEAR * m)
            for n in range(3):
                total = total + cnear[h, n, t].astype(F32)
            if m:
                fsend[h, m] = total.astype(BF)
                launch(fsend.at[h, m], cfar.at[h, m], fs.at[h], fr.at[h], chip(NEAR * m))
        last[h] = total
    for h in range(2):
        total = last[h]
        wait_received(cfar.at[h, others], fr.at[h])
        for m in range(1, K):
            total = total + cfar[h, m].astype(F32)
        dbuf[h, r, c, k] = total.astype(BF)
        far_step(dbuf.at[h], d_sem.at[h], late, 0, h == 0)
    gather_sent(abuf, a_sem)
    wait_sent(abuf.at[:, 0], a_sem.at[2])
    wait_sent(hsend.at[pl.ds(0, N - 1)], hs)
    wait_sent(hsum.at[pl.ds(0, N - 1)], gs)
    wait_sent(sibf, ss)
    wait_sent(csend, ns)
    for h in range(2):
        wait_sent(fsend.at[h, others], fs.at[h])
    eloc[:, :, 20:24, :] = jnp.zeros((2, 2, 4, 512), F32)
    far_gather(*((dbuf.at[h], d_sem.at[h], late, h == 0) for h in range(2)))

    def adapter_part(h, a):
        x = dbuf[h, :, a].reshape(2 * rows, 256)
        eloc[h, a, 0:20, 0:256] = dot_nn(f0, x)
        eloc[h, a, 0:20, 256:512] = dot_nn(f1, x)
        launch(eloc.at[h, a], erem.at[h, a], es, er.at[h, a], peer)

    for h in range(2):
        near_gather(dbuf.at[h], d_sem.at[h])
        adapter_part(h, c)
        from_other_core(dbuf.at[h], d_sem.at[h])
        adapter_part(h, 1 - c)
    for h in range(2):
        gather_sent(dbuf.at[h], d_sem.at[h])
        wait_sent(dbuf.at[h, :, 0], d_sem.at[h, 2])
        for a in range(2):
            blk = dbuf[h, r, a, k].astype(F32)
            for e in range(2):
                block8 = blk[8 * e : 8 * e + 8]
                at = 1024 * a + 512 * h + 256 * e
                ig_out[:, at : at + 256] = jnp.where(c == 0, block8[0:4], block8[4:8])
    for h in range(2):
        for a in range(2):
            wait_received(erem.at[h, a], er.at[h, a])
            at = 1024 * a + 512 * h
            ad_out[:, at : at + 512] = eloc[h, a, 0:20, :] + erem[h, a, 0:20, :]
    wait_sent(eloc, es)


def finish(ig, ad, ig_out, ad_out):
    ig_out[...] = ig[...].astype(BF)
    ad_out[...] = ad[...]


def per_device(Z, N, out_grad, gate_act, up_act, frames, w_gate, w_up, w_down):
    K = Z // NEAR
    hbm = pl.BlockSpec(memory_space=pl.ANY)
    vmem = pl.BlockSpec(memory_space=pltpu.VMEM)
    dma = pltpu.SemaphoreType.DMA
    ig, ad = pl.pallas_call(
        functools.partial(body, Z, N),
        out_shape=(jax.ShapeDtypeStruct((4, 2048), F32), jax.ShapeDtypeStruct((20, 2048), F32)),
        in_specs=[vmem, hbm, hbm, vmem, hbm, hbm, hbm],
        out_specs=(vmem, vmem),
        scratch_shapes=[
            pltpu.VMEM((NEAR, 2, K, 16, 512), BF),
            pltpu.VMEM((2, NEAR, 2, K, 16, 256), BF),
            pltpu.VMEM((256, 2048), BF),
            pltpu.VMEM((N, 32, 512), F32),
            pltpu.VMEM((N, 32, 512), BF),
            pltpu.VMEM((N - 1, 32, 512), BF),
            pltpu.VMEM((N, 32, 512), BF),
            pltpu.VMEM((N, 32, 512), F32),
            pltpu.VMEM((N, 32, 512), F32),
            pltpu.VMEM((2, N, 32, 512), BF),
            pltpu.VMEM((256, 512), BF),
            pltpu.VMEM((256, 512), BF),
            pltpu.VMEM((2048, 512), BF),
            pltpu.VMEM((2048, 512), BF),
            pltpu.VMEM((512, 2048), BF),
            pltpu.VMEM((2, Z, 8, 512), F32),
            pltpu.VMEM((2, Z, 8, 512), F32),
            pltpu.VMEM((2, Z, 8, 512), F32),
            pltpu.VMEM((2, 3, K, 16, 256), BF),
            pltpu.VMEM((2, 3, K, 16, 256), BF),
            pltpu.VMEM((2, K, 16, 256), BF),
            pltpu.VMEM((2, K, 16, 256), BF),
            pltpu.VMEM((2, 2, 24, 512), F32),
            pltpu.VMEM((2, 2, 24, 512), F32),
            dma((5,)),
            dma((18,)),
            dma((2, 18)),
            dma,
            dma,
            dma,
            dma,
            dma,
            dma((2,)),
            dma,
            dma((2, 3)),
            dma((2,)),
            dma((2,)),
            dma,
            dma((2, 2)),
        ],
        compiler_params=pltpu.CompilerParams(
            collective_id=0, has_side_effects=True, vmem_limit_bytes=60 * 1024 * 1024
        ),
        cost_estimate=pl.CostEstimate(flops=1_700_000_000, bytes_accessed=8_000_000, transcendentals=0),
    )(out_grad, gate_act, up_act, frames.T, w_gate, w_up, w_down)
    return pl.pallas_call(
        finish,
        out_shape=(jax.ShapeDtypeStruct((4, 2048), BF), jax.ShapeDtypeStruct((20, 2048), F32)),
        in_specs=[vmem, vmem],
        out_specs=(vmem, vmem),
        compiler_params=pltpu.CompilerParams(vmem_limit_bytes=60 * 1024 * 1024),
    )(ig, ad)


def solution(mesh):
    Z = mesh.shape["hid"] // 2
    N = mesh.shape["inp"]
    return jax.shard_map(
        functools.partial(per_device, Z, N),
        mesh=mesh,
        in_specs=(
            P(("dp", "hid"), "inp"),
            P("dp", "hid"),
            P("dp", "hid"),
            P("dp", "hid"),
            P("inp", "hid"),
            P("inp", "hid"),
            P("hid", "inp"),
        ),
        out_specs=(P(("dp", "hid"), "inp"), P("hid", "inp")),
        check_vma=False,
    )
```

```python
import functools

import jax
import jax.numpy as jnp
from jax import lax
from jax.experimental import pallas as pl
from jax.experimental.pallas import tpu as pltpu
from jax.sharding import PartitionSpec as P

MESH = pl.DeviceIdType.MESH
BF = jnp.bfloat16
F32 = jnp.float32
NEAR = 4


def dot_nt(a, b):
    return lax.dot_general(a, b, (((1,), (1,)), ((), ())), preferred_element_type=F32)


def dot_nn(a, b):
    return lax.dot_general(a, b, (((1,), (0,)), ((), ())), preferred_element_type=F32)


def body(Z, N, *refs):
    (og, gact, uact, frames, wg, wu, wd, ig_out, ad_out,
     abuf, dbuf, full, hpart, hsend, hrecv, hsum, gate_by, up_by, gu, gact_v, uact_v, wg_v, wu_v, wd_v,
     sibf, sibr, pown, csend, cnear, fsend, cfar, eloc, erem,
     lsem, a_sem, d_sem, hs, hr, gs, gr, ss, sr, ns, nr, fs, fr, es, er) = refs
    K = Z // NEAR
    hid = lax.axis_index("hid")
    z = hid // 2
    c = hid % 2
    inp = lax.axis_index("inp")
    dp = lax.axis_index("dp")
    r = z % NEAR
    k = z // NEAR
    sib = {"hid": 2 * z + 1 - c}
    peer = {"dp": 1 - dp}

    def chip(d):
        return {"hid": 2 * ((z + d + 2 * Z) % Z) + c}

    def chip_at(w):
        return {"hid": 2 * w + c}

    def ring(j):
        return {"inp": (inp + j) % N}

    barrier = pltpu.get_barrier_semaphore()
    offsets = (NEAR, Z - NEAR, 1, Z - 1, 2, Z - 2)
    for d in offsets:
        pl.semaphore_signal(barrier, inc=1, device_id=chip(d), device_id_type=MESH)
    for j in range(1, N):
        pl.semaphore_signal(barrier, inc=1, device_id=ring(j), device_id_type=MESH)
    pl.semaphore_signal(barrier, inc=1, device_id=sib, device_id_type=MESH)
    pl.semaphore_signal(barrier, inc=1, device_id=peer, device_id_type=MESH)

    local = [
        pltpu.make_async_copy(wd, wd_v, lsem.at[0]),
        pltpu.make_async_copy(gact, gact_v, lsem.at[1]),
        pltpu.make_async_copy(uact, uact_v, lsem.at[2]),
        pltpu.make_async_copy(wg, wg_v, lsem.at[3]),
        pltpu.make_async_copy(wu, wu_v, lsem.at[4]),
    ]
    for q in local:
        q.start()

    rows4 = og[...].astype(F32)
    abuf[r, c, k] = jnp.concatenate(
        [rows4[:, 512 * q : 512 * q + 512] for q in range(4)], axis=0
    ).astype(BF)
    pl.semaphore_wait(barrier, len(offsets) + N + 1)

    def remote(s, d, send, recv, dev):
        return pltpu.make_async_remote_copy(
            src_ref=s, dst_ref=d, send_sem=send, recv_sem=recv, device_id=dev, device_id_type=MESH
        )

    def launch(*args):
        remote(*args).start()

    def wait_sent(ref, sem):
        remote(ref, ref, sem, sem, sib).wait_send()

    def wait_received(ref, sem):
        remote(ref, ref, sem, sem, sib).wait_recv()

    two = 2 - 4 * c
    near = (two, 1, -1)
    arrivals = ((1, -1), (2, -2), (3, -3, 4))
    early = {1: (0, 0, 1), -1: (0, 0, -1), 2: (1, 1, 1), -2: (-1, -1, -1),
             3: (-1, 1, 2), -3: (-1, -1, -2), 4: (2, 2, 2)}
    late = {4: (0, 0, 4), 1: (0, 0, 1), -1: (0, 0, -1), 2: (1, 1, 1), -2: (-1, -1, -1),
            3: (2, 2, 1), -3: (-2, -2, -1)}

    def far_step(buf, sem, tree, m, whole=False):
        for to, (after, held, step) in tree.items():
            if after == m:
                blk = buf.at[r, c, (k - held + K) % K]
                launch(blk, blk, sem.at[0], sem.at[10 + to % K], chip(NEAR * step))
        if not whole:
            near_step(buf.at[r, c, (k - m + K) % K], sem)

    def near_step(blk, sem):
        for n, d in enumerate(near):
            launch(blk, blk, sem.at[1], sem.at[3 + n], chip(d))

    def far_gather(*chains):
        for wave in arrivals:
            for buf, sem, tree, whole in chains:
                for m in wave:
                    wait_received(buf.at[r, c, (k - m + K) % K], sem.at[10 + m % K])
                    far_step(buf, sem, tree, m, whole)
                if wave is arrivals[-1]:
                    group = buf.at[r, c]
                    if whole:
                        near_step(group, sem)
                    launch(group, group, sem.at[2], sem.at[9], sib)

    def near_gather(buf, sem):
        for n, d in ((1, 1), (2, -1), (0, two)):
            got = buf.at[(r - d + NEAR) % NEAR, c]
            wait_received(got, sem.at[3 + n])
            launch(got, got, sem.at[2], sem.at[6 + n], sib)

    def from_other_core(buf, sem):
        for n, d in ((3, 0), (1, 1), (2, -1), (0, 2)):
            wait_received(buf.at[(r - d + NEAR) % NEAR, 1 - c], sem.at[6 + n])

    def gather_sent(buf, sem):
        wait_sent(buf.at[0, 0, pl.ds(0, K - 1)], sem.at[0])
        wait_sent(buf.at[pl.ds(0, 3), 0], sem.at[1])

    far_step(abuf, a_sem, early, 0)

    o = lax.broadcasted_iota(jnp.int32, (256, 256), 0)
    i = lax.broadcasted_iota(jnp.int32, (256, 256), 1)
    to = ((i // 4) % 4) * 64 + ((i // 16) % 2) * 32 + (i // 64) * 8 + ((i // 32) % 2) * 4 + i % 4
    perm = jnp.where(o == to, 1.0, 0.0).astype(BF)
    rows = Z * 8
    row = lax.broadcasted_iota(jnp.int32, (rows, 2 * rows), 0)
    col = lax.broadcasted_iota(jnp.int32, (rows, 2 * rows), 1)
    src = 8 * (NEAR * ((col // 16) % K) + col // (16 * K)) + col % 8
    half = (col // 8) % 2
    fr_t = frames[...]
    f0 = dot_nn(fr_t, jnp.where((row == src) & (half == 0), 1.0, 0.0).astype(BF)).astype(BF)
    f1 = dot_nn(fr_t, jnp.where((row == src) & (half == 1), 1.0, 0.0).astype(BF)).astype(BF)

    local[1].wait()
    local[2].wait()
    for t in range(N):
        part32 = pl.ds(32 * t, 32)
        gate = gact_v[part32].astype(F32)
        upper = uact_v[part32].astype(F32)
        sigma = jax.nn.sigmoid(gate)
        gate_by[t] = upper * sigma * (1.0 + gate * (1.0 - sigma))
        up_by[t] = gate * sigma
    far_gather((abuf, a_sem, early, False))
    near_gather(abuf, a_sem)
    from_other_core(abuf, a_sem)

    for j in range(K // 2):
        rows_in = abuf[:, :, 2 * j : 2 * j + 2].reshape(256, 512)
        out = dot_nn(perm, rows_in).astype(BF)
        for q in range(4):
            full[64 * j : 64 * j + 64, 512 * q : 512 * q + 512] = out[64 * q : 64 * q + 64]
    local[0].wait()
    for g in range(2):
        hpart[g] = dot_nt(full[...], wd_v[256 * g : 256 * g + 256, :]).reshape(N, 32, 256)
        hsend[g] = hpart[g].astype(BF)
        for j in range(1, N):
            launch(hsend.at[g, (inp + j) % N], hrecv.at[g, j - 1], hs.at[g], hr.at[g], ring(j))
    for g in range(2):
        total = hpart[g, inp]
        wait_received(hrecv.at[g], hr.at[g])
        for j in range(1, N):
            total = total + hrecv[g, j - 1].astype(F32)
        hsum[g, inp] = total.astype(BF)
        for j in range(1, N):
            launch(hsum.at[g, inp], hsum.at[g, inp], gs.at[g], gr.at[g], ring(j))

    def grads(g, t):
        h = hsum[g, t].astype(F32)
        cols = pl.ds(256 * g, 256)
        gu[0, t, :, cols] = (h * gate_by[t, :, cols]).astype(BF)
        gu[1, t, :, cols] = (h * up_by[t, :, cols]).astype(BF)

    local[3].wait()
    local[4].wait()
    for g in range(2):
        grads(g, inp)
        wait_received(hsum.at[g, pl.ds(0, N - 1)], gr.at[g])
        for j in range(1, N):
            grads(g, (inp - j + N) % N)

    gg = gu[0].reshape(256, 512)
    ug = gu[1].reshape(256, 512)

    def part(start):
        w = pl.ds(pl.multiple_of(start, 512), 512)
        return (dot_nt(gg, wg_v[w, :]) + dot_nt(ug, wu_v[w, :])).reshape(Z, 8, 512)

    order = sorted(range(K), key=lambda m: -min(m, K - m))

    def rows_of(h, w):
        own = pown[h, (w + 2 * Z) % Z]
        return jnp.concatenate([own[:, 0:256], own[:, 256:512]], axis=0)

    for h in range(2):
        sibf[h] = part((1 - c) * 1024 + h * 512)
        launch(sibf.at[h], sibr.at[h], ss, sr.at[h], sib)
        pown[h] = part(c * 1024 + h * 512)
        wait_received(sibr.at[h], sr.at[h])
        pown[h] = pown[h] + sibr[h]
        for n, d in enumerate(near):
            for t in range(K):
                csend[h, n, t] = rows_of(h, z + d + NEAR * order[t]).astype(BF)
            launch(csend.at[h, n], cnear.at[h, n], ns, nr.at[h, n], chip(d))
    others = pl.ds(1, K - 1)
    last = [None, None]
    for h in range(2):
        for n in (1, 2, 0):
            wait_received(cnear.at[h, n], nr.at[h, n])
        for t in range(K):
            m = order[t]
            total = rows_of(h, z + NEAR * m)
            for n in range(3):
                total = total + cnear[h, n, t].astype(F32)
            if m:
                fsend[h, m] = total.astype(BF)
                launch(fsend.at[h, m], cfar.at[h, m], fs.at[h], fr.at[h], chip(NEAR * m))
        last[h] = total
    for h in range(2):
        total = last[h]
        wait_received(cfar.at[h, others], fr.at[h])
        for m in range(1, K):
            total = total + cfar[h, m].astype(F32)
        dbuf[h, r, c, k] = total.astype(BF)
        far_step(dbuf.at[h], d_sem.at[h], late, 0, h == 0)
    gather_sent(abuf, a_sem)
    wait_sent(abuf.at[:, 0], a_sem.at[2])
    for g in range(2):
        wait_sent(hsend.at[g, pl.ds(0, N - 1)], hs.at[g])
        wait_sent(hsum.at[g, pl.ds(0, N - 1)], gs.at[g])
    wait_sent(sibf, ss)
    wait_sent(csend, ns)
    for h in range(2):
        wait_sent(fsend.at[h, others], fs.at[h])
    eloc[:, :, 20:24, :] = jnp.zeros((2, 2, 4, 512), F32)
    far_gather(*((dbuf.at[h], d_sem.at[h], late, h == 0) for h in range(2)))

    def adapter_part(h, a):
        x = dbuf[h, :, a].reshape(2 * rows, 256)
        eloc[h, a, 0:20, 0:256] = dot_nn(f0, x)
        eloc[h, a, 0:20, 256:512] = dot_nn(f1, x)
        launch(eloc.at[h, a], erem.at[h, a], es, er.at[h, a], peer)

    for h in range(2):
        near_gather(dbuf.at[h], d_sem.at[h])
        adapter_part(h, c)
        from_other_core(dbuf.at[h], d_sem.at[h])
        adapter_part(h, 1 - c)
    for h in range(2):
        gather_sent(dbuf.at[h], d_sem.at[h])
        wait_sent(dbuf.at[h, :, 0], d_sem.at[h, 2])
        for a in range(2):
            blk = dbuf[h, r, a, k].astype(F32)
            for e in range(2):
                block8 = blk[8 * e : 8 * e + 8]
                at = 1024 * a + 512 * h + 256 * e
                ig_out[:, at : at + 256] = jnp.where(c == 0, block8[0:4], block8[4:8])
    for h in range(2):
        for a in range(2):
            wait_received(erem.at[h, a], er.at[h, a])
            at = 1024 * a + 512 * h
            ad_out[:, at : at + 512] = eloc[h, a, 0:20, :] + erem[h, a, 0:20, :]
    wait_sent(eloc, es)


def finish(ig, ad, ig_out, ad_out):
    ig_out[...] = ig[...].astype(BF)
    ad_out[...] = ad[...]


def per_device(Z, N, out_grad, gate_act, up_act, frames, w_gate, w_up, w_down):
    K = Z // NEAR
    hbm = pl.BlockSpec(memory_space=pl.ANY)
    vmem = pl.BlockSpec(memory_space=pltpu.VMEM)
    dma = pltpu.SemaphoreType.DMA
    ig, ad = pl.pallas_call(
        functools.partial(body, Z, N),
        out_shape=(jax.ShapeDtypeStruct((4, 2048), F32), jax.ShapeDtypeStruct((20, 2048), F32)),
        in_specs=[vmem, hbm, hbm, vmem, hbm, hbm, hbm],
        out_specs=(vmem, vmem),
        scratch_shapes=[
            pltpu.VMEM((NEAR, 2, K, 16, 512), BF),
            pltpu.VMEM((2, NEAR, 2, K, 16, 256), BF),
            pltpu.VMEM((256, 2048), BF),
            pltpu.VMEM((2, N, 32, 256), F32),
            pltpu.VMEM((2, N, 32, 256), BF),
            pltpu.VMEM((2, N - 1, 32, 256), BF),
            pltpu.VMEM((2, N, 32, 256), BF),
            pltpu.VMEM((N, 32, 512), F32),
            pltpu.VMEM((N, 32, 512), F32),
            pltpu.VMEM((2, N, 32, 512), BF),
            pltpu.VMEM((256, 512), BF),
            pltpu.VMEM((256, 512), BF),
            pltpu.VMEM((2048, 512), BF),
            pltpu.VMEM((2048, 512), BF),
            pltpu.VMEM((512, 2048), BF),
            pltpu.VMEM((2, Z, 8, 512), F32),
            pltpu.VMEM((2, Z, 8, 512), F32),
            pltpu.VMEM((2, Z, 8, 512), F32),
            pltpu.VMEM((2, 3, K, 16, 256), BF),
            pltpu.VMEM((2, 3, K, 16, 256), BF),
            pltpu.VMEM((2, K, 16, 256), BF),
            pltpu.VMEM((2, K, 16, 256), BF),
            pltpu.VMEM((2, 2, 24, 512), F32),
            pltpu.VMEM((2, 2, 24, 512), F32),
            dma((5,)),
            dma((18,)),
            dma((2, 18)),
            dma((2,)),
            dma((2,)),
            dma((2,)),
            dma((2,)),
            dma,
            dma((2,)),
            dma,
            dma((2, 3)),
            dma((2,)),
            dma((2,)),
            dma,
            dma((2, 2)),
        ],
        compiler_params=pltpu.CompilerParams(
            collective_id=0, has_side_effects=True, vmem_limit_bytes=60 * 1024 * 1024
        ),
        cost_estimate=pl.CostEstimate(flops=1_700_000_000, bytes_accessed=8_000_000, transcendentals=0),
    )(out_grad, gate_act, up_act, frames.T, w_gate, w_up, w_down)
    return pl.pallas_call(
        finish,
        out_shape=(jax.ShapeDtypeStruct((4, 2048), BF), jax.ShapeDtypeStruct((20, 2048), F32)),
        in_specs=[vmem, vmem],
        out_specs=(vmem, vmem),
        compiler_params=pltpu.CompilerParams(vmem_limit_bytes=60 * 1024 * 1024),
    )(ig, ad)


def solution(mesh):
    Z = mesh.shape["hid"] // 2
    N = mesh.shape["inp"]
    return jax.shard_map(
        functools.partial(per_device, Z, N),
        mesh=mesh,
        in_specs=(
            P(("dp", "hid"), "inp"),
            P("dp", "hid"),
            P("dp", "hid"),
            P("dp", "hid"),
            P("inp", "hid"),
            P("inp", "hid"),
            P("hid", "inp"),
        ),
        out_specs=(P(("dp", "hid"), "inp"), P("hid", "inp")),
        check_vma=False,
    )
```

```python
import functools

import jax
import jax.numpy as jnp
from jax import lax
from jax.experimental import pallas as pl
from jax.experimental.pallas import tpu as pltpu
from jax.sharding import PartitionSpec as P

MESH = pl.DeviceIdType.MESH
BF = jnp.bfloat16
F32 = jnp.float32
NEAR = 4


def dot_nt(a, b):
    return lax.dot_general(a, b, (((1,), (1,)), ((), ())), preferred_element_type=F32)


def dot_nn(a, b):
    return lax.dot_general(a, b, (((1,), (0,)), ((), ())), preferred_element_type=F32)


def body(Z, N, *refs):
    (og, gact, uact, frames, wg, wu, wd, ig_out, ad_out,
     abuf, dbuf, full, hpart, hsend, hrecv, hsum, gate_by, up_by, gu, gact_v, uact_v, wg_v, wu_v, wd_v,
     sibf, sibr, pown, csend, cnear, fsend, cfar, eloc, erem,
     lsem, a_sem, d_sem, hs, hr, gs, gr, ss, sr, ns, nr, fs, fr, es, er) = refs
    K = Z // NEAR
    hid = lax.axis_index("hid")
    z = hid // 2
    c = hid % 2
    inp = lax.axis_index("inp")
    dp = lax.axis_index("dp")
    r = z % NEAR
    k = z // NEAR
    sib = {"hid": 2 * z + 1 - c}
    peer = {"dp": 1 - dp}

    def chip(d):
        return {"hid": 2 * ((z + d + 2 * Z) % Z) + c}

    def chip_at(w):
        return {"hid": 2 * w + c}

    def ring(j):
        return {"inp": (inp + j) % N}

    barrier = pltpu.get_barrier_semaphore()
    offsets = (NEAR, Z - NEAR, 1, Z - 1, 2, Z - 2)
    for d in offsets:
        pl.semaphore_signal(barrier, inc=1, device_id=chip(d), device_id_type=MESH)
    for j in range(1, N):
        pl.semaphore_signal(barrier, inc=1, device_id=ring(j), device_id_type=MESH)
    pl.semaphore_signal(barrier, inc=1, device_id=sib, device_id_type=MESH)
    pl.semaphore_signal(barrier, inc=1, device_id=peer, device_id_type=MESH)

    local = [
        pltpu.make_async_copy(wd, wd_v, lsem.at[0]),
        pltpu.make_async_copy(gact, gact_v, lsem.at[1]),
        pltpu.make_async_copy(uact, uact_v, lsem.at[2]),
        pltpu.make_async_copy(wg, wg_v, lsem.at[3]),
        pltpu.make_async_copy(wu, wu_v, lsem.at[4]),
    ]
    for q in local:
        q.start()

    rows4 = og[...].astype(F32)
    abuf[r, c, k] = jnp.concatenate(
        [rows4[:, 512 * q : 512 * q + 512] for q in range(4)], axis=0
    ).astype(BF)
    pl.semaphore_wait(barrier, len(offsets) + N + 1)

    def remote(s, d, send, recv, dev):
        return pltpu.make_async_remote_copy(
            src_ref=s, dst_ref=d, send_sem=send, recv_sem=recv, device_id=dev, device_id_type=MESH
        )

    def launch(*args):
        remote(*args).start()

    def wait_sent(ref, sem):
        remote(ref, ref, sem, sem, sib).wait_send()

    def wait_received(ref, sem):
        remote(ref, ref, sem, sem, sib).wait_recv()

    two = 2 - 4 * c
    near = (two, 1, -1)
    arrivals = ((1, -1), (2, -2), (3, -3, 4))
    early = {1: (0, 0, 1), -1: (0, 0, -1), 2: (1, 1, 1), -2: (-1, -1, -1),
             3: (-1, 1, 2), -3: (-1, -1, -2), 4: (2, 2, 2)}
    late = {4: (0, 0, 4), 1: (0, 0, 1), -1: (0, 0, -1), 2: (1, 1, 1), -2: (-1, -1, -1),
            3: (2, 2, 1), -3: (-2, -2, -1)}

    def far_step(buf, sem, tree, m, whole=False):
        for to, (after, held, step) in tree.items():
            if after == m:
                blk = buf.at[r, c, (k - held + K) % K]
                launch(blk, blk, sem.at[0], sem.at[10 + to % K], chip(NEAR * step))
        if not whole:
            near_step(buf.at[r, c, (k - m + K) % K], sem)

    def near_step(blk, sem):
        for n, d in enumerate(near):
            launch(blk, blk, sem.at[1], sem.at[3 + n], chip(d))

    def far_gather(*chains):
        for wave in arrivals:
            for buf, sem, tree, whole in chains:
                for m in wave:
                    wait_received(buf.at[r, c, (k - m + K) % K], sem.at[10 + m % K])
                    far_step(buf, sem, tree, m, whole)
                if wave is arrivals[-1]:
                    group = buf.at[r, c]
                    if whole:
                        near_step(group, sem)
                    launch(group, group, sem.at[2], sem.at[9], sib)

    def near_gather(buf, sem):
        for n, d in ((1, 1), (2, -1), (0, two)):
            got = buf.at[(r - d + NEAR) % NEAR, c]
            wait_received(got, sem.at[3 + n])
            launch(got, got, sem.at[2], sem.at[6 + n], sib)

    def from_other_core(buf, sem):
        for n, d in ((3, 0), (1, 1), (2, -1), (0, 2)):
            wait_received(buf.at[(r - d + NEAR) % NEAR, 1 - c], sem.at[6 + n])

    def gather_sent(buf, sem):
        wait_sent(buf.at[0, 0, pl.ds(0, K - 1)], sem.at[0])
        wait_sent(buf.at[pl.ds(0, 3), 0], sem.at[1])

    far_step(abuf, a_sem, early, 0)

    o = lax.broadcasted_iota(jnp.int32, (256, 256), 0)
    i = lax.broadcasted_iota(jnp.int32, (256, 256), 1)
    to = ((i // 4) % 4) * 64 + ((i // 16) % 2) * 32 + (i // 64) * 8 + ((i // 32) % 2) * 4 + i % 4
    perm = jnp.where(o == to, 1.0, 0.0).astype(BF)
    rows = Z * 8
    row = lax.broadcasted_iota(jnp.int32, (rows, 2 * rows), 0)
    col = lax.broadcasted_iota(jnp.int32, (rows, 2 * rows), 1)
    src = 8 * (NEAR * ((col // 16) % K) + col // (16 * K)) + col % 8
    half = (col // 8) % 2
    fr_t = frames[...]
    f0 = dot_nn(fr_t, jnp.where((row == src) & (half == 0), 1.0, 0.0).astype(BF)).astype(BF)
    f1 = dot_nn(fr_t, jnp.where((row == src) & (half == 1), 1.0, 0.0).astype(BF)).astype(BF)

    local[1].wait()
    local[2].wait()
    for t in range(N):
        part32 = pl.ds(32 * t, 32)
        gate = gact_v[part32].astype(F32)
        upper = uact_v[part32].astype(F32)
        sigma = jax.nn.sigmoid(gate)
        gate_by[t] = upper * sigma * (1.0 + gate * (1.0 - sigma))
        up_by[t] = gate * sigma
    far_gather((abuf, a_sem, early, False))
    near_gather(abuf, a_sem)
    from_other_core(abuf, a_sem)

    for j in range(K // 2):
        rows_in = abuf[:, :, 2 * j : 2 * j + 2].reshape(256, 512)
        out = dot_nn(perm, rows_in).astype(BF)
        for q in range(4):
            full[64 * j : 64 * j + 64, 512 * q : 512 * q + 512] = out[64 * q : 64 * q + 64]
    local[0].wait()
    for g in range(2):
        hpart[g] = dot_nt(full[...], wd_v[256 * g : 256 * g + 256, :]).reshape(N, 32, 256)
        hsend[g] = hpart[g].astype(BF)
        for j in range(1, N):
            launch(hsend.at[g, (inp + j) % N], hrecv.at[g, j - 1], hs.at[g], hr.at[g], ring(j))
    for g in range(2):
        total = hpart[g, inp]
        wait_received(hrecv.at[g], hr.at[g])
        for j in range(1, N):
            total = total + hrecv[g, j - 1].astype(F32)
        hsum[g, inp] = total.astype(BF)
        for j in range(1, N):
            launch(hsum.at[g, inp], hsum.at[g, inp], gs.at[g], gr.at[g], ring(j))

    def grads(g, t):
        h = hsum[g, t].astype(F32)
        cols = pl.ds(256 * g, 256)
        gu[0, t, :, cols] = (h * gate_by[t, :, cols]).astype(BF)
        gu[1, t, :, cols] = (h * up_by[t, :, cols]).astype(BF)

    def part(start, g):
        w = pl.ds(pl.multiple_of(start, 512), 512)
        cols = pl.ds(256 * g, 256)
        gg = gu[0, :, :, cols].reshape(256, 256)
        ug = gu[1, :, :, cols].reshape(256, 256)
        return (dot_nt(gg, wg_v[w, cols]) + dot_nt(ug, wu_v[w, cols])).reshape(Z, 8, 512)

    local[3].wait()
    local[4].wait()
    for g in range(2):
        grads(g, inp)
        wait_received(hsum.at[g, pl.ds(0, N - 1)], gr.at[g])
        for j in range(1, N):
            grads(g, (inp - j + N) % N)
        if g == 0:
            sibf[0] = part((1 - c) * 1024, 0)
            pown[0] = part(c * 1024, 0)

    order = sorted(range(K), key=lambda m: -min(m, K - m))

    def rows_of(h, w):
        own = pown[h, (w + 2 * Z) % Z]
        return jnp.concatenate([own[:, 0:256], own[:, 256:512]], axis=0)

    for h in range(2):
        away, here = (1 - c) * 1024 + h * 512, c * 1024 + h * 512
        sibf[h] = part(away, 1) + (sibf[h] if h == 0 else part(away, 0))
        launch(sibf.at[h], sibr.at[h], ss, sr.at[h], sib)
        pown[h] = part(here, 1) + (pown[h] if h == 0 else part(here, 0))
        wait_received(sibr.at[h], sr.at[h])
        pown[h] = pown[h] + sibr[h]
        for n, d in enumerate(near):
            for t in range(K):
                csend[h, n, t] = rows_of(h, z + d + NEAR * order[t]).astype(BF)
            launch(csend.at[h, n], cnear.at[h, n], ns, nr.at[h, n], chip(d))
    others = pl.ds(1, K - 1)
    last = [None, None]
    for h in range(2):
        for n in (1, 2, 0):
            wait_received(cnear.at[h, n], nr.at[h, n])
        for t in range(K):
            m = order[t]
            total = rows_of(h, z + NEAR * m)
            for n in range(3):
                total = total + cnear[h, n, t].astype(F32)
            if m:
                fsend[h, m] = total.astype(BF)
                launch(fsend.at[h, m], cfar.at[h, m], fs.at[h], fr.at[h], chip(NEAR * m))
        last[h] = total
    for h in range(2):
        total = last[h]
        wait_received(cfar.at[h, others], fr.at[h])
        for m in range(1, K):
            total = total + cfar[h, m].astype(F32)
        dbuf[h, r, c, k] = total.astype(BF)
        far_step(dbuf.at[h], d_sem.at[h], late, 0, h == 0)
    gather_sent(abuf, a_sem)
    wait_sent(abuf.at[:, 0], a_sem.at[2])
    for g in range(2):
        wait_sent(hsend.at[g, pl.ds(0, N - 1)], hs.at[g])
        wait_sent(hsum.at[g, pl.ds(0, N - 1)], gs.at[g])
    wait_sent(sibf, ss)
    wait_sent(csend, ns)
    for h in range(2):
        wait_sent(fsend.at[h, others], fs.at[h])
    eloc[:, :, 20:24, :] = jnp.zeros((2, 2, 4, 512), F32)
    far_gather(*((dbuf.at[h], d_sem.at[h], late, h == 0) for h in range(2)))

    def adapter_part(h, a):
        x = dbuf[h, :, a].reshape(2 * rows, 256)
        eloc[h, a, 0:20, 0:256] = dot_nn(f0, x)
        eloc[h, a, 0:20, 256:512] = dot_nn(f1, x)
        launch(eloc.at[h, a], erem.at[h, a], es, er.at[h, a], peer)

    for h in range(2):
        near_gather(dbuf.at[h], d_sem.at[h])
        adapter_part(h, c)
        from_other_core(dbuf.at[h], d_sem.at[h])
        adapter_part(h, 1 - c)
    for h in range(2):
        gather_sent(dbuf.at[h], d_sem.at[h])
        wait_sent(dbuf.at[h, :, 0], d_sem.at[h, 2])
        for a in range(2):
            blk = dbuf[h, r, a, k].astype(F32)
            for e in range(2):
                block8 = blk[8 * e : 8 * e + 8]
                at = 1024 * a + 512 * h + 256 * e
                ig_out[:, at : at + 256] = jnp.where(c == 0, block8[0:4], block8[4:8])
    for h in range(2):
        for a in range(2):
            wait_received(erem.at[h, a], er.at[h, a])
            at = 1024 * a + 512 * h
            ad_out[:, at : at + 512] = eloc[h, a, 0:20, :] + erem[h, a, 0:20, :]
    wait_sent(eloc, es)


def finish(ig, ad, ig_out, ad_out):
    ig_out[...] = ig[...].astype(BF)
    ad_out[...] = ad[...]


def per_device(Z, N, out_grad, gate_act, up_act, frames, w_gate, w_up, w_down):
    K = Z // NEAR
    hbm = pl.BlockSpec(memory_space=pl.ANY)
    vmem = pl.BlockSpec(memory_space=pltpu.VMEM)
    dma = pltpu.SemaphoreType.DMA
    ig, ad = pl.pallas_call(
        functools.partial(body, Z, N),
        out_shape=(jax.ShapeDtypeStruct((4, 2048), F32), jax.ShapeDtypeStruct((20, 2048), F32)),
        in_specs=[vmem, hbm, hbm, vmem, hbm, hbm, hbm],
        out_specs=(vmem, vmem),
        scratch_shapes=[
            pltpu.VMEM((NEAR, 2, K, 16, 512), BF),
            pltpu.VMEM((2, NEAR, 2, K, 16, 256), BF),
            pltpu.VMEM((256, 2048), BF),
            pltpu.VMEM((2, N, 32, 256), F32),
            pltpu.VMEM((2, N, 32, 256), BF),
            pltpu.VMEM((2, N - 1, 32, 256), BF),
            pltpu.VMEM((2, N, 32, 256), BF),
            pltpu.VMEM((N, 32, 512), F32),
            pltpu.VMEM((N, 32, 512), F32),
            pltpu.VMEM((2, N, 32, 512), BF),
            pltpu.VMEM((256, 512), BF),
            pltpu.VMEM((256, 512), BF),
            pltpu.VMEM((2048, 512), BF),
            pltpu.VMEM((2048, 512), BF),
            pltpu.VMEM((512, 2048), BF),
            pltpu.VMEM((2, Z, 8, 512), F32),
            pltpu.VMEM((2, Z, 8, 512), F32),
            pltpu.VMEM((2, Z, 8, 512), F32),
            pltpu.VMEM((2, 3, K, 16, 256), BF),
            pltpu.VMEM((2, 3, K, 16, 256), BF),
            pltpu.VMEM((2, K, 16, 256), BF),
            pltpu.VMEM((2, K, 16, 256), BF),
            pltpu.VMEM((2, 2, 24, 512), F32),
            pltpu.VMEM((2, 2, 24, 512), F32),
            dma((5,)),
            dma((18,)),
            dma((2, 18)),
            dma((2,)),
            dma((2,)),
            dma((2,)),
            dma((2,)),
            dma,
            dma((2,)),
            dma,
            dma((2, 3)),
            dma((2,)),
            dma((2,)),
            dma,
            dma((2, 2)),
        ],
        compiler_params=pltpu.CompilerParams(
            collective_id=0, has_side_effects=True, vmem_limit_bytes=60 * 1024 * 1024
        ),
        cost_estimate=pl.CostEstimate(flops=1_700_000_000, bytes_accessed=8_000_000, transcendentals=0),
    )(out_grad, gate_act, up_act, frames.T, w_gate, w_up, w_down)
    return pl.pallas_call(
        finish,
        out_shape=(jax.ShapeDtypeStruct((4, 2048), BF), jax.ShapeDtypeStruct((20, 2048), F32)),
        in_specs=[vmem, vmem],
        out_specs=(vmem, vmem),
        compiler_params=pltpu.CompilerParams(vmem_limit_bytes=60 * 1024 * 1024),
    )(ig, ad)


def solution(mesh):
    Z = mesh.shape["hid"] // 2
    N = mesh.shape["inp"]
    return jax.shard_map(
        functools.partial(per_device, Z, N),
        mesh=mesh,
        in_specs=(
            P(("dp", "hid"), "inp"),
            P("dp", "hid"),
            P("dp", "hid"),
            P("dp", "hid"),
            P("inp", "hid"),
            P("inp", "hid"),
            P("hid", "inp"),
        ),
        out_specs=(P(("dp", "hid"), "inp"), P("hid", "inp")),
        check_vma=False,
    )
```
